512 devices in a mesh: gx: 8 (over y_hi, x), gy: 8 (over y_lo, core), gz: 8 (over z).
Axes of the slice: x: 4, y: 8 (y_hi: 2, y_lo: 4; y = y_hi * 4 + y_lo), z: 8, core: 2. Of those that a mesh axis runs over, the one named last changes fastest.
Arguments:
- inputs: bfloat16 [2048, 6144], P('gx', ('gy', 'gz')), may hold values from -6 to 6
- out_grad: bfloat16 [2048, 6144], P('gx', ('gy', 'gz')), may hold values from -3 to 3
- w_in: bfloat16 [6144, 16384], P('gy', ('gx', 'gz')), may hold values from -0.078125 to 0.078125
- w_out: bfloat16 [16384, 6144], P(('gx', 'gz'), 'gy'), may hold values from -0.046875 to 0.046875
Outputs:
- input_grad: bfloat16 [2048, 6144], P('gx', ('gy', 'gz'))
- weight_grad: bfloat16 [6144, 16384], P('gy', ('gx', 'gz'))
- gram_out: float32 [8, 6144, 768], P('gz', ('gy', 'gx'))
The draws below stay inside these ranges and needn't reach their ends.
All inputs are finite; a program needn't handle non-finite values.
Results may differ from the reference program's by a relative error of at most 0.027.
Values may be sent and summed in bfloat16 or wider, within the bound.
A program may use at most 64 MiB of HBM per device.

```python
import jax
import jax.numpy as jnp
from jax import lax

D = 6144
FW = 16384
TOK_DEV = 256
TOKENS = 2048
BR = 768
CB = 256
N_GX = 8
N_GY = 8
N_GZ = 8


def level_of(rng, dims, cuts, least, top_value):
    factor_of = 1.0
    for position, blocks in cuts:
        steps = jax.random.uniform(jax.random.fold_in(jax.random.fold_in(rng, 6), position), (blocks,), jnp.float32, least / len(cuts), top_value / len(cuts))
        factor_of = factor_of * jnp.repeat(jnp.exp(steps), dims[position] // blocks).reshape((-1,) + (1,) * (len(dims) - 1 - position))
    return factor_of


def centred(own_key, shape, scale, most, cuts=(), kind=jnp.bfloat16):
    loudness = level_of(own_key, shape, cuts, -0.22, 0.18) if cuts else 1.0
    entries = jax.random.normal(own_key, shape, jnp.float32) * scale * loudness
    return jnp.minimum(jnp.maximum(entries, -most), most).astype(kind)


def setup_inputs(seed: int = 0) -> dict:
    key_list = jax.random.split(jax.random.key(seed), 5)
    inputs = centred(key_list[0], (TOKENS, D), 1.0, 6.0, ((0, 8), (1, 64)))
    out_grad = centred(key_list[1], (TOKENS, D), 0.5, 3.0, ((0, 8), (1, 64)))
    w_in = centred(key_list[2], (D, FW), D ** -0.5, 0.078125, ((0, 8), (1, 64)))
    w_out = centred(key_list[3], (FW, D), FW ** -0.5, 0.046875, ((0, 64), (1, 8)))
    return {"inputs": inputs, "out_grad": out_grad, "w_in": w_in, "w_out": w_out}


GELU_COEF = 0.7978845608

def gelu_slope(preact):
    inner = GELU_COEF * (preact + 0.044715 * preact * preact * preact)
    tanh_part = jnp.tanh(inner)
    return 0.5 * (1.0 + tanh_part) + 0.5 * preact * (1.0 - tanh_part * tanh_part) * GELU_COEF * (1.0 + 3.0 * 0.044715 * preact * preact)

def rounded(value):
    return lax.optimization_barrier(value.astype(jnp.bfloat16)).astype(jnp.float32)

def reference(inputs, out_grad, w_in, w_out):
    feat_span = D // N_GY
    hidden_pre = jnp.zeros((TOKENS, FW), jnp.float32)
    hidden_back = jnp.zeros((TOKENS, FW), jnp.float32)
    for y in range(N_GY):
        low = y * feat_span
        high = low + feat_span
        hidden_pre = hidden_pre + rounded(jnp.dot(inputs[:, low:high], w_in[low:high, :], preferred_element_type=jnp.float32))
        hidden_back = hidden_back + rounded(jnp.dot(out_grad[:, low:high], w_out[:, low:high].T, preferred_element_type=jnp.float32))
    hidden_grad = (hidden_back * gelu_slope(hidden_pre)).astype(jnp.bfloat16)
    input_grad = jnp.dot(hidden_grad, w_in.T, preferred_element_type=jnp.float32).astype(jnp.bfloat16)
    weight_sum = jnp.zeros((D, FW), jnp.float32)
    for b in range(N_GX):
        low = b * TOK_DEV
        high = low + TOK_DEV
        weight_sum = weight_sum + rounded(jnp.dot(inputs[low:high, :].T, hidden_grad[low:high, :], preferred_element_type=jnp.float32))
    weight_grad = weight_sum.astype(jnp.bfloat16)
    blocks = weight_grad.reshape(N_GY, BR, N_GX, N_GZ, CB)
    gram_groups = []
    for z in range(N_GZ):
        gram_rows = []
        for y in range(N_GY):
            grad_block = blocks[y, :, :, z, :].reshape(BR, N_GX * CB).astype(jnp.float32)
            block_sq = jnp.sum(grad_block * grad_block)
            factor = 1.0 / (jnp.sqrt(block_sq) + 1e-07)
            normed = (grad_block * factor).astype(jnp.bfloat16)
            gram_rows.append(jnp.float32(BR) * jnp.dot(normed, normed.T, preferred_element_type=jnp.float32))
        gram_groups.append(jnp.concatenate(gram_rows, axis=0))
    gram_out = jnp.stack(gram_groups, axis=0)
    return (input_grad, weight_grad, gram_out)
```

```python
import jax
import jax.numpy as jnp
from jax import lax
from jax.experimental import pallas as pl
from jax.experimental.pallas import tpu as pltpu
from jax.sharding import PartitionSpec as P

GELU_COEF = 0.7978845608
BF = jnp.bfloat16
F32 = jnp.float32
MESH = pl.DeviceIdType.MESH
UP = float(2.0**30)
DOWN = float(2.0**-30)


def gelu_slope(preact):
    inner = GELU_COEF * (preact + 0.044715 * preact * preact * preact)
    tanh_part = jnp.tanh(inner)
    return 0.5 * (1.0 + tanh_part) + 0.5 * preact * (1.0 - tanh_part * tanh_part) * GELU_COEF * (
        1.0 + 3.0 * 0.044715 * preact * preact
    )


def dot(a, b, ca, cb):
    return lax.dot_general(a, b, (((ca,), (cb,)), ((), ())), preferred_element_type=F32)


def kernel(
    xg_in, win, wout, dx_out, dw_out, gram_out,
    xg, wi_g, wo_g, psend, pown, crecv, ysend, yrecv, ht,
    dxacc, dxs, dxr, dxh, dxhr, dwf1, dwf3, dws, dwr, dwfin,
    gbuf, gsend, grecv, ghs, ghr, sqs, sqr,
    s_h, s_z, r_z, s_w, r_w, s_c, r_c, s_y, r_y, s_ah, r_ah, s_ac, r_ac,
    s_dw, r_dw, s_dx, r_dx, s_dxh, s_g, r_g, s_gh, s_sq, r_sq,
):
    gx = lax.axis_index("gx")
    gy = lax.axis_index("gy")
    z = lax.axis_index("gz")
    hi, xx = gx // 4, gx % 4
    yy, cc = gy // 2, gy % 2
    xp, xm = hi * 4 + (xx + 1) % 4, hi * 4 + (xx + 3) % 4
    other_hi = (1 - hi) * 4 + xx
    other_core = yy * 2 + 1 - cc
    zp, zm = (z + 1) % 8, (z + 7) % 8

    barrier = pltpu.get_barrier_semaphore()
    for k in range(1, 8):
        pl.semaphore_signal(barrier, inc=1, device_id={"gx": (gx + k) % 8}, device_id_type=MESH)
        pl.semaphore_signal(barrier, inc=1, device_id={"gz": (z + k) % 8}, device_id_type=MESH)
    for k in range(1, 4):
        pl.semaphore_signal(
            barrier, inc=1, device_id={"gy": ((yy + k) % 4) * 2 + cc}, device_id_type=MESH
        )
    pl.semaphore_signal(barrier, inc=1, device_id={"gy": other_core}, device_id_type=MESH)
    pl.semaphore_wait(barrier, 18)

    started = []

    def rc(src, dst, ssem, rsem, dev):
        return pltpu.make_async_remote_copy(
            src_ref=src, dst_ref=dst, send_sem=ssem, recv_sem=rsem,
            device_id=dev, device_id_type=MESH,
        )

    def send(src, dst, ssem, rsem, dev):
        copy = rc(src, dst, ssem, rsem, dev)
        copy.start()
        started.append(copy)

    def zrows(i):
        return pl.ds(pl.multiple_of(i * 96, 32), 96)

    own = zrows(z)
    h_dev = {"gx": other_hi}
    send(xg_in, xg.at[:, 1, own, :], s_h.at[0], s_h.at[1], h_dev)
    hops = ((4, 3), (3, 4))

    def zcopy(r, a, d, s, at=None):
        dev = zp if d == 0 else zm
        begun = (z + 8 - (s - 1)) % 8 if d == 0 else (z + s - 1) % 8
        rows = zrows(begun)
        src = xg.at[a, r, rows, :]
        if s == 1 and r == 0:
            src = xg_in.at[a]
        return src, xg.at[a, r, rows, :], s_z.at[r, a, d, s - 1], r_z.at[r, a, d, s - 1], {"gz": dev}

    def zwait(r, a, d, s):
        begun = (z + 8 - s) % 8 if d == 0 else (z + s) % 8
        rows = zrows(begun)
        ref = xg.at[a, r, rows, :]
        rc(ref, ref, s_z.at[r, a, d, s - 1], r_z.at[r, a, d, s - 1], {"gz": zp}).wait_recv()

    for a in range(2):
        for d in range(2):
            send(*zcopy(0, a, d, 1))
    send(win, wi_g.at[2], s_w.at[0], r_w.at[0], {"gx": xp})
    send(wout, wo_g.at[2], s_w.at[1], r_w.at[1], {"gx": xp})
    send(win, wi_g.at[0], s_w.at[2], r_w.at[2], {"gx": xm})
    send(wout, wo_g.at[0], s_w.at[3], r_w.at[3], {"gx": xm})
    xg[:, 0, own, :] = xg_in[...]

    rc(xg_in, xg.at[:, 1, own, :], s_h.at[0], s_h.at[1], h_dev).wait_recv()
    for a in range(2):
        for d in range(2):
            send(*zcopy(1, a, d, 1))
    for s in range(1, 5):
        for r in range(2):
            for a in range(2):
                for d in range(2):
                    if s <= hops[a][d]:
                        zwait(r, a, d, s)
                        if s < hops[a][d]:
                            send(*zcopy(r, a, d, s + 1))

    def wait_w(i):
        ref = (wi_g, wo_g)[i % 2].at[2 if i < 2 else 0]
        rc(ref, ref, s_w.at[i], r_w.at[i], {"gx": xp}).wait_recv()

    wait_w(2)
    wait_w(3)
    def w_of(c):
        return (win, wout) if c == 3 else (wi_g.at[c], wo_g.at[c])

    def half(i):
        return pl.ds(pl.multiple_of(i * 128, 128), 128)

    c_dev = {"gy": other_core}

    def part(c, side):
        wi, wo = w_of(c)
        wi_h = wi[:, half(side)]
        wo_h = wo[half(side), :]
        return [
            [dot(wi_h, xg[0, r], 0, 0) for r in range(2)],
            [dot(wo_h, xg[1, r], 1, 0) for r in range(2)],
        ]

    def stage_a(c):
        vals = part(c, 1 - cc)
        for k in range(2):
            for r in range(2):
                psend[c, k, r] = vals[k][r].astype(BF)
        send(psend.at[c], crecv.at[c], s_c.at[c], r_c.at[c], c_dev)
        vals = part(c, cc)
        for k in range(2):
            for r in range(2):
                pown[c, k, r] = vals[k][r]

    def yrows(i):
        return pl.ds(pl.multiple_of(i * 32, 32), 32)

    def stage_b(c):
        rc(psend.at[c], crecv.at[c], s_c.at[c], r_c.at[c], c_dev).wait_recv()
        total = pown[c] + crecv[c].astype(F32)
        pown[c] = total
        ysend[c] = total.astype(BF)
        for k in (1, 3, 2):
            to = (yy + k) % 4
            send(
                ysend.at[c, :, :, yrows(to), :], yrecv.at[c, k - 1],
                s_y.at[c, k - 1], r_y.at[c, k - 1], {"gy": to * 2 + cc},
            )

    def hrows(y):
        return pl.ds(pl.multiple_of(cc * 128 + y * 32, 32), 32)

    def stage_c(c):
        total = pown[c, :, :, yrows(yy), :]
        for k in range(1, 4):
            ref = yrecv.at[c, k - 1]
            rc(ref, ref, s_y.at[c, k - 1], r_y.at[c, k - 1], c_dev).wait_recv()
            total = total + yrecv[c, k - 1].astype(F32)
        ht[c, :, hrows(yy), :] = (total[1] * gelu_slope(total[0])).astype(BF)
        for k in (1, 3, 2):
            to = (yy + k) % 4
            ref = ht.at[c, :, hrows(yy), :]
            send(ref, ref, s_ah.at[c, k - 1], r_ah.at[c, k - 1], {"gy": to * 2 + cc})

    def stage_d(c):
        for k in range(1, 4):
            ref = ht.at[c, :, hrows((yy + 4 - k) % 4), :]
            rc(ref, ref, s_ah.at[c, k - 1], r_ah.at[c, k - 1], c_dev).wait_recv()
        ref = ht.at[c, :, half(cc), :]
        send(ref, ref, s_ac.at[c], r_ac.at[c], c_dev)

    def wait_dw(i, ref):
        rc(ref, ref, s_dw.at[i], r_dw.at[i], {"gx": xp}).wait_recv()

    def stage_e(c):
        ref = ht.at[c, :, half(1 - cc), :]
        rc(ref, ref, s_ac.at[c], r_ac.at[c], c_dev).wait_recv()
        wi = w_of(c)[0]
        for r in range(2):
            val = dot(wi[...], ht[c, r], 1, 0)
            dxacc[r] = val if c == 0 else dxacc[r] + val
        if c == 3:
            dxs[...] = dxacc[...].astype(BF)
            for k in (4, 3, 5, 2, 6, 1, 7):
                to = (z + k) % 8
                send(
                    dxs.at[:, zrows(to), :], dxr.at[k - 1],
                    s_dx.at[k - 1], r_dx.at[k - 1], {"gz": to},
                )
        dw = dot(xg[0, 0], ht[c, 0], 1, 1) + dot(xg[0, 1], ht[c, 1], 1, 1)
        if c == 0:
            dwf1[...] = dw[:384]
            dws[2] = dw[384:].astype(BF)
            send(dws.at[2], dwr.at[2], s_dw.at[2], r_dw.at[2], {"gx": xp})
        elif c == 1:
            dws[0] = dw[:384].astype(BF)
            dws[1] = dw[384:].astype(BF)
            send(dws.at[0], dwr.at[0], s_dw.at[0], r_dw.at[0], {"gx": xp})
            send(dws.at[1], dwr.at[1], s_dw.at[1], r_dw.at[1], {"gx": xm})
        elif c == 2:
            dws[3] = dw[:384].astype(BF)
            send(dws.at[3], dwr.at[3], s_dw.at[3], r_dw.at[3], {"gx": xm})
            dwf3[...] = dw[384:]
            wait_dw(0, dwr.at[0])
            dws[4] = (dwf1[...] + dwr[0].astype(F32)).astype(BF)
            send(dws.at[4], dwr.at[4], s_dw.at[4], r_dw.at[4], {"gx": xp})
            wait_dw(1, dwr.at[1])
            dws[5] = (dwf3[...] + dwr[1].astype(F32)).astype(BF)
            send(dws.at[5], dwr.at[5], s_dw.at[5], r_dw.at[5], {"gx": xm})
        else:
            for i in (2, 3, 4, 5):
                wait_dw(i, dwr.at[i])
            low = dw[:384] + dwr[3].astype(F32) + dwr[4].astype(F32)
            high = dw[384:] + dwr[2].astype(F32) + dwr[5].astype(F32)
            dwfin[:384, :] = low.astype(BF)
            dwfin[384:, :] = high.astype(BF)

    stage_a(0)
    wait_w(0)
    wait_w(1)
    send(wi_g.at[2], wi_g.at[1], s_w.at[4], r_w.at[4], {"gx": xp})
    send(wo_g.at[0], wo_g.at[1], s_w.at[5], r_w.at[5], {"gx": xm})
    stage_b(0)

    def wait_opposite():
        rc(wi_g.at[2], wi_g.at[1], s_w.at[4], r_w.at[4], {"gx": xp}).wait_recv()
        rc(wo_g.at[0], wo_g.at[1], s_w.at[5], r_w.at[5], {"gx": xm}).wait_recv()

    wait_opposite()
    stage_a(1)
    stage_b(1)
    stage_a(2)
    stage_b(2)
    stage_c(0)
    stage_a(3)
    stage_b(3)
    stage_d(0)
    stage_c(1)
    stage_e(0)
    stage_d(1)
    stage_c(2)
    stage_e(1)
    stage_d(2)
    stage_c(3)
    stage_e(2)
    stage_d(3)
    stage_e(3)

    w = dwfin[...]
    dw_out[...] = w
    wf = w.astype(F32)
    sqs[...] = jnp.broadcast_to(jnp.sum(wf * wf), (8, 128))
    for k in range(1, 8):
        send(sqs, sqr.at[k - 1], s_sq.at[k - 1], r_sq.at[k - 1], {"gx": (gx + k) % 8})
    ws = (wf * UP).astype(BF)
    gbuf[...] = dot(ws, ws, 1, 1).reshape(2, 4, 96, 768)
    x1, x2, x3 = (xx + 1) % 4, (xx + 2) % 4, (xx + 3) % 4

    def wait_g(i):
        rc(gsend.at[i], grecv.at[i], s_g.at[i], r_g.at[i], {"gx": xp}).wait_recv()

    def send_g(i, val, dev):
        gsend[i] = val.astype(BF)
        send(gsend.at[i], grecv.at[i], s_g.at[i], r_g.at[i], {"gx": dev})

    send_g(0, gbuf[0, x2], xp)
    send_g(1, gbuf[1, x2], xm)
    send_g(2, gbuf[1, x1], xp)
    send_g(3, gbuf[0, x3], xm)
    wait_g(0)
    send_g(4, gbuf[0, x1] + grecv[0].astype(F32), xp)
    wait_g(1)
    send_g(5, gbuf[1, x3] + grecv[1].astype(F32), xm)

    dx_tot = [dxacc[0, own, :], dxacc[1, own, :]]
    for k in (1, 7, 2, 6, 3, 5, 4):
        ref = dxr.at[k - 1]
        rc(ref, ref, s_dx.at[k - 1], r_dx.at[k - 1], c_dev).wait_recv()
        for r in range(2):
            dx_tot[r] = dx_tot[r] + dxr[k - 1, r].astype(F32)
    dxh[...] = dx_tot[1].astype(BF)
    send(dxh, dxhr, s_dxh.at[0], s_dxh.at[1], h_dev)

    for i in (2, 3, 4, 5):
        wait_g(i)
    gbuf[0, xx] = gbuf[0, xx] + grecv[3].astype(F32) + grecv[4].astype(F32)
    gbuf[1, xx] = gbuf[1, xx] + grecv[2].astype(F32) + grecv[5].astype(F32)
    ghs[...] = gbuf[1 - hi, xx].astype(BF)
    send(ghs, ghr, s_gh.at[0], s_gh.at[1], h_dev)

    rc(dxh, dxhr, s_dxh.at[0], s_dxh.at[1], h_dev).wait_recv()
    dx_out[...] = (dx_tot[0] + dxhr[...].astype(F32)).astype(BF)

    sq = sqs[...]
    for k in range(1, 8):
        rc(sqs, sqr.at[k - 1], s_sq.at[k - 1], r_sq.at[k - 1], h_dev).wait_recv()
        sq = sq + sqr[k - 1]
    factor = DOWN / (jnp.sqrt(sq[:1, :1]) + 1e-07)
    rc(ghs, ghr, s_gh.at[0], s_gh.at[1], h_dev).wait_recv()
    gram_out[...] = (gbuf[hi, xx] + ghr[...].astype(F32)) * factor * factor * 768.0

    for copy in started:
        copy.wait_send()


def body(inputs, out_grad, w_in, w_out):
    xg_in = jnp.stack([inputs.T, out_grad.T])
    vmem = pl.BlockSpec(memory_space=pltpu.VMEM)
    dma = pltpu.SemaphoreType.DMA
    dx_t, weight_grad, gram = pl.pallas_call(
        kernel,
        out_shape=(
            jax.ShapeDtypeStruct((96, 256), BF),
            jax.ShapeDtypeStruct((768, 256), BF),
            jax.ShapeDtypeStruct((96, 768), F32),
        ),
        in_specs=[vmem] * 3,
        out_specs=(vmem,) * 3,
        scratch_shapes=[
            pltpu.VMEM((2, 2, 768, 256), BF),
            pltpu.VMEM((3, 768, 256), BF),
            pltpu.VMEM((3, 256, 768), BF),
            pltpu.VMEM((4, 2, 2, 128, 256), BF),
            pltpu.VMEM((4, 2, 2, 128, 256), F32),
            pltpu.VMEM((4, 2, 2, 128, 256), BF),
            pltpu.VMEM((4, 2, 2, 128, 256), BF),
            pltpu.VMEM((4, 3, 2, 2, 32, 256), BF),
            pltpu.VMEM((4, 2, 256, 256), BF),
            pltpu.VMEM((2, 768, 256), F32),
            pltpu.VMEM((2, 768, 256), BF),
            pltpu.VMEM((7, 2, 96, 256), BF),
            pltpu.VMEM((96, 256), BF),
            pltpu.VMEM((96, 256), BF),
            pltpu.VMEM((384, 256), F32),
            pltpu.VMEM((384, 256), F32),
            pltpu.VMEM((6, 384, 256), BF),
            pltpu.VMEM((6, 384, 256), BF),
            pltpu.VMEM((768, 256), BF),
            pltpu.VMEM((2, 4, 96, 768), F32),
            pltpu.VMEM((6, 96, 768), BF),
            pltpu.VMEM((6, 96, 768), BF),
            pltpu.VMEM((96, 768), BF),
            pltpu.VMEM((96, 768), BF),
            pltpu.VMEM((8, 128), F32),
            pltpu.VMEM((7, 8, 128), F32),
            dma((2,)), dma((2, 2, 2, 4)), dma((2, 2, 2, 4)), dma((6,)), dma((6,)),
            dma((4,)), dma((4,)), dma((4, 3)), dma((4, 3)), dma((4, 3)), dma((4, 3)),
            dma((4,)), dma((4,)), dma((6,)), dma((6,)), dma((7,)), dma((7,)), dma((2,)),
            dma((6,)), dma((6,)), dma((2,)), dma((7,)), dma((7,)),
        ],
        compiler_params=pltpu.CompilerParams(
            collective_id=0, has_side_effects=True, vmem_limit_bytes=48 * 1024 * 1024
        ),
        cost_estimate=pl.CostEstimate(
            flops=3_600_000_000, bytes_accessed=4_000_000, transcendentals=131072
        ),
    )(xg_in, w_in, w_out)
    return (dx_t.T, weight_grad, gram[None])


def solution(mesh):
    placed = (
        P("gx", ("gy", "gz")),
        P("gx", ("gy", "gz")),
        P("gy", ("gx", "gz")),
        P(("gx", "gz"), "gy"),
    )
    return jax.shard_map(
        body,
        mesh=mesh,
        in_specs=placed,
        out_specs=(P("gx", ("gy", "gz")), P("gy", ("gx", "gz")), P("gz", ("gy", "gx"), None)),
        check_vma=False,
    )
```

```python
import jax
import jax.numpy as jnp
from jax import lax
from jax.experimental import pallas as pl
from jax.experimental.pallas import tpu as pltpu
from jax.sharding import PartitionSpec as P

GELU_COEF = 0.7978845608
BF = jnp.bfloat16
F32 = jnp.float32
MESH = pl.DeviceIdType.MESH
UP = float(2.0**30)
DOWN = float(2.0**-30)
NH = 2
CH = 256 // NH
NP = 3
SLOTS = 288

ORDER = [
    (0, 0, 0), (0, 1, 0), (1, 0, 0), (3, 0, 0), (1, 0, 1), (3, 0, 1), (1, 1, 0), (3, 1, 0),
    (1, 1, 1), (3, 1, 1), (2, 0, 0), (2, 0, 1), (2, 1, 0), (2, 1, 1), (0, 0, 1), (0, 1, 1),
]
LAG_B, LAG_B2, LAG_C, LAG_D, LAG_E = 1, 3, 5, 7, 8


def gelu_slope(preact):
    inner = GELU_COEF * (preact + 0.044715 * preact * preact * preact)
    tanh_part = jnp.tanh(inner)
    return 0.5 * (1.0 + tanh_part) + 0.5 * preact * (1.0 - tanh_part * tanh_part) * GELU_COEF * (
        1.0 + 3.0 * 0.044715 * preact * preact
    )


def dot(a, b, ca, cb):
    return lax.dot_general(a, b, (((ca,), (cb,)), ((), ())), preferred_element_type=F32)


def kernel(
    x_in, g_in, win, wout, dx_out, dw_out, gram_out,
    xin, xg, wi, wo, psend, pown, crecv, ysend, yrecv, y2send, y2recv, ht,
    dxacc, dxs, dxr, dxh, dxhr, dwf, dwf0, dws, dwr,
    gbuf, gsend, grecv, ghs, ghr, sqs, sqr, l_sem, s_all, r_all,
):
    gx = lax.axis_index("gx")
    gy = lax.axis_index("gy")
    z = lax.axis_index("gz")
    hi, xx = gx // 4, gx % 4
    yy, cc = gy // 2, gy % 2
    b0, b1 = yy % 2, yy // 2
    xp = {"gx": hi * 4 + (xx + 1) % 4}
    xm = {"gx": hi * 4 + (xx + 3) % 4}
    h_dev = {"gx": (1 - hi) * 4 + xx}
    c_dev = {"gy": yy * 2 + 1 - cc}
    y1_dev = {"gy": (b1 * 2 + 1 - b0) * 2 + cc}
    y2_dev = {"gy": ((1 - b1) * 2 + b0) * 2 + cc}
    y3_dev = {"gy": ((1 - b1) * 2 + 1 - b0) * 2 + cc}
    zp, zm = {"gz": (z + 1) % 8}, {"gz": (z + 7) % 8}

    barrier = pltpu.get_barrier_semaphore()
    partners = [{"gx": (gx + k) % 8} for k in range(1, 8)]
    partners += [{"gz": (z + k) % 8} for k in range(1, 8)]
    partners += [c_dev, y1_dev, y2_dev, y3_dev]
    for dev in partners:
        pl.semaphore_signal(barrier, inc=1, device_id=dev, device_id_type=MESH)

    slots = {}
    started = []

    def rc(src, dst, name, dev):
        slot = slots.setdefault(name, len(slots))
        return pltpu.make_async_remote_copy(
            src_ref=src, dst_ref=dst, send_sem=s_all.at[slot], recv_sem=r_all.at[slot],
            device_id=dev, device_id_type=MESH,
        )

    def send(src, dst, name, dev):
        copy = rc(src, dst, name, dev)
        copy.start()
        started.append(copy)

    def arrived(ref, name):
        rc(ref, ref, name, c_dev).wait_recv()

    def zrows(i):
        return pl.ds(pl.multiple_of(i * 96, 32), 96)

    own = zrows(z)
    local = [
        pltpu.make_async_copy(x_in, xin.at[0], l_sem.at[0]),
        pltpu.make_async_copy(g_in, xin.at[1], l_sem.at[1]),
        pltpu.make_async_copy(win, wi.at[0], l_sem.at[2]),
        pltpu.make_async_copy(wout, wo.at[0], l_sem.at[3]),
    ]
    for copy in local:
        copy.start()
    for a in range(2):
        local[a].wait()
        xg[a, 0, own, :] = xin[a].T
    pl.semaphore_wait(barrier, len(partners))

    hops = ((4, 3), (3, 4))

    def zref(r, a, d, s):
        begun = (z + 8 - s) % 8 if d == 0 else (z + s) % 8
        return xg.at[a, r, zrows(begun), :]

    def zsend(r, a, d, s):
        ref = zref(r, a, d, s - 1)
        send(ref, ref, ("z", r, a, d, s), zp if d == 0 else zm)

    def zstep(r, s):
        for a in range(2):
            for d in range(2):
                if s <= hops[a][d]:
                    arrived(zref(r, a, d, s), ("z", r, a, d, s))
                    if s < hops[a][d]:
                        zsend(r, a, d, s + 1)

    def hstep():
        for a in range(2):
            arrived(xg.at[a, 1, own, :], ("h", a))
            for d in range(2):
                zsend(1, a, d, 1)

    for a in range(2):
        send(xg.at[a, 0, own, :], xg.at[a, 1, own, :], ("h", a), h_dev)
        for d in range(2):
            zsend(0, a, d, 1)

    def piece(b):
        return pl.ds(b * CH, CH)

    for b in range(NH):
        send(win.at[:, piece(b)], wi.at[3, :, piece(b)], ("w", b, 0), xp)
        send(win.at[:, piece(b)], wi.at[1, :, piece(b)], ("w", b, 2), xm)
        send(wout.at[piece(b), :], wo.at[3, piece(b), :], ("w", b, 1), xp)
        send(wout.at[piece(b), :], wo.at[1, piece(b), :], ("w", b, 3), xm)

    def w_near(b):
        arrived(wi.at[3, :, piece(b)], ("w", b, 0))
        send(wi.at[3, :, piece(b)], wi.at[2, :, piece(b)], ("w", b, 4), xp)
        arrived(wo.at[1, piece(b), :], ("w", b, 3))
        send(wo.at[1, piece(b), :], wo.at[2, piece(b), :], ("w", b, 5), xm)
        arrived(wi.at[1, :, piece(b)], ("w", b, 2))
        arrived(wo.at[3, piece(b), :], ("w", b, 1))

    def w_far(b):
        arrived(wi.at[2, :, piece(b)], ("w", b, 4))
        arrived(wo.at[2, piece(b), :], ("w", b, 5))

    zstep(0, 1)
    hstep()
    zstep(0, 2)
    zstep(1, 1)
    zstep(0, 3)
    zstep(0, 4)
    local[2].wait()
    local[3].wait()

    def rows(i, n):
        return pl.ds(pl.multiple_of(i * n, n), n)

    def stage_a(c):
        s, b, r = ORDER[c]
        pre = dot(wi[s, :, b * CH : (b + 1) * CH], xg[0, r], 0, 0)
        back = dot(wo[s, b * CH : (b + 1) * CH, :], xg[1, r], 1, 0)
        for k, val in enumerate((pre, back)):
            pown[c, k] = val
            psend[c, k] = val.astype(BF)
        send(psend.at[c, :, rows(1 - cc, CH // 2), :], crecv.at[c], ("c", c), c_dev)

    def stage_b(c):
        arrived(crecv.at[c], ("c", c))
        total = pown[c, :, rows(cc, CH // 2), :] + crecv[c].astype(F32)
        pown[c, :, : CH // 2, :] = total
        ysend[c] = total.astype(BF)
        send(ysend.at[c, :, rows(1 - b0, CH // 4), :], yrecv.at[c], ("y", c), y1_dev)

    def stage_b2(c):
        arrived(yrecv.at[c], ("y", c))
        total = pown[c, :, rows(b0, CH // 4), :] + yrecv[c].astype(F32)
        pown[c, :, : CH // 4, :] = total
        y2send[c] = total.astype(BF)
        send(y2send.at[c, :, rows(1 - b1, CH // 8), :], y2recv.at[c], ("y2", c), y2_dev)

    def hrows(p0, p1):
        return rows(cc * 4 + p0 * 2 + p1, CH // 8)

    def stage_c(c):
        arrived(y2recv.at[c], ("y2", c))
        total = pown[c, :, rows(b1, CH // 8), :] + y2recv[c].astype(F32)
        ht[c, hrows(b0, b1), :] = (total[1] * gelu_slope(total[0])).astype(BF)
        ref = ht.at[c, hrows(b0, b1), :]
        for k, dev in ((1, y1_dev), (2, y2_dev), (3, y3_dev)):
            send(ref, ref, ("ah", c, k), dev)

    def stage_d(c):
        arrived(ht.at[c, hrows(1 - b0, b1), :], ("ah", c, 1))
        arrived(ht.at[c, hrows(b0, 1 - b1), :], ("ah", c, 2))
        arrived(ht.at[c, hrows(1 - b0, 1 - b1), :], ("ah", c, 3))
        ref = ht.at[c, rows(cc, CH // 2), :]
        send(ref, ref, ("ac", c), c_dev)

    done = set()
    seen = [0, 0]

    def stage_e(c):
        s, b, r = ORDER[c]
        arrived(ht.at[c, rows(1 - cc, CH // 2), :], ("ac", c))
        val = dot(wi[s, :, b * CH : (b + 1) * CH], ht[c], 1, 0)
        dxacc[r] = val if seen[r] == 0 else dxacc[r] + val
        seen[r] += 1
        if seen[r] == 4 * NH:
            dxs[r] = dxacc[r].astype(BF)
            for k in (4, 3, 5, 2, 6, 1, 7):
                to = (z + k) % 8
                send(dxs.at[r, zrows(to), :], dxr.at[r, k - 1], ("dx", r, k), {"gz": to})
        done.add((s, b, r))
        if (s, b, 1 - r) not in done:
            return
        c0, c1 = ORDER.index((s, b, 0)), ORDER.index((s, b, 1))
        dw = dot(xg[0, 0], ht[c0], 1, 1) + dot(xg[0, 1], ht[c1], 1, 1)
        if s == 0:
            dwf0[b] = dw
        elif s == 1:
            dwf[b, 0] = dw[:384]
            put_dw(b, 2, dw[384:], xp)
        elif s == 2:
            put_dw(b, 0, dw[:384], xp)
            put_dw(b, 1, dw[384:], xm)
        else:
            dwf[b, 1] = dw[384:]
            put_dw(b, 3, dw[:384], xm)

    def put_dw(b, i, val, dev):
        dws[b, i] = val.astype(BF)
        send(dws.at[b, i], dwr.at[b, i], ("dw", b, i), dev)

    def add_dw(b):
        for i, dev in ((0, xp), (1, xm)):
            arrived(dwr.at[b, i], ("dw", b, i))
            put_dw(b, 4 + i, dwf[b, i] + dwr[b, i].astype(F32), dev)

    def own_dw(b):
        for i in (2, 3, 4, 5):
            arrived(dwr.at[b, i], ("dw", b, i))
        low = dwf0[b, :384] + dwr[b, 3].astype(F32) + dwr[b, 4].astype(F32)
        high = dwf0[b, 384:] + dwr[b, 2].astype(F32) + dwr[b, 5].astype(F32)
        dw_out[:384, b * CH : (b + 1) * CH] = low.astype(BF)
        dw_out[384:, b * CH : (b + 1) * CH] = high.astype(BF)

    before = {1: [lambda: zstep(1, 2)], 2: [lambda: w_near(0), lambda: zstep(1, 3)],
              4: [lambda: zstep(1, 4)], 6: [lambda: w_near(1)], 10: [lambda: w_far(0)], 12: [lambda: w_far(1)]}
    after = {13: [lambda: add_dw(0)], 14: [lambda: add_dw(1)]}
    n = len(ORDER)
    for tick in range(n + LAG_E):
        for lag, stage in ((0, stage_a), (LAG_B, stage_b), (LAG_B2, stage_b2), (LAG_C, stage_c), (LAG_D, stage_d), (LAG_E, stage_e)):
            c = tick - lag
            if 0 <= c < n:
                if lag == 0:
                    for act in before.get(c, ()):
                        act()
                stage(c)
                if lag == LAG_E:
                    for act in after.get(c, ()):
                        act()
    for b in range(NH):
        own_dw(b)

    wf = dw_out[...].astype(F32)
    sqs[...] = jnp.broadcast_to(jnp.sum(wf * wf), (8, 128))
    for k in range(1, 8):
        send(sqs, sqr.at[k - 1], ("sq", k), {"gx": (gx + k) % 8})
    ws = (wf * UP).astype(BF)
    x1, x2, x3 = (xx + 1) % 4, (xx + 2) % 4, (xx + 3) % 4
    width = 768 // NP

    def put_g(p, i, val, dev):
        gsend[p, i] = val.astype(BF)
        send(gsend.at[p, i], grecv.at[p, i], ("g", p, i), dev)

    def gram_part(p):
        gbuf[p] = dot(ws, ws[p * width : (p + 1) * width], 1, 1).reshape(2, 4, 96, width)
        put_g(p, 0, gbuf[p, 0, x2], xp)
        put_g(p, 1, gbuf[p, 1, x2], xm)
        put_g(p, 2, gbuf[p, 1, x1], xp)
        put_g(p, 3, gbuf[p, 0, x3], xm)

    def gram_add(p):
        arrived(grecv.at[p, 0], ("g", p, 0))
        put_g(p, 4, gbuf[p, 0, x1] + grecv[p, 0].astype(F32), xp)
        arrived(grecv.at[p, 1], ("g", p, 1))
        put_g(p, 5, gbuf[p, 1, x3] + grecv[p, 1].astype(F32), xm)

    def gram_own(p):
        for i in (2, 3, 4, 5):
            arrived(grecv.at[p, i], ("g", p, i))
        gbuf[p, 0, xx] = gbuf[p, 0, xx] + grecv[p, 3].astype(F32) + grecv[p, 4].astype(F32)
        gbuf[p, 1, xx] = gbuf[p, 1, xx] + grecv[p, 2].astype(F32) + grecv[p, 5].astype(F32)
        ghs[p] = gbuf[p, 1 - hi, xx].astype(BF)
        send(ghs.at[p], ghr.at[p], ("gh", p), h_dev)

    def dx_sum(r):
        total = dxacc[r, own, :]
        for k in (1, 7, 2, 6, 3, 5, 4):
            arrived(dxr.at[r, k - 1], ("dx", r, k))
            total = total + dxr[r, k - 1].astype(F32)
        return total

    gram_part(0)
    gram_part(1)
    gram_add(0)
    gram_part(2)
    gram_add(1)
    gram_add(2)
    gram_own(0)
    dxh[...] = dx_sum(1).astype(BF)
    send(dxh, dxhr, ("dxh",), h_dev)
    gram_own(1)
    gram_own(2)
    dx_own = dx_sum(0)
    arrived(dxhr, ("dxh",))
    dx_out[...] = (dx_own + dxhr[...].astype(F32)).astype(BF)

    sq = sqs[...]
    for k in range(1, 8):
        arrived(sqr.at[k - 1], ("sq", k))
        sq = sq + sqr[k - 1]
    factor = DOWN / (jnp.sqrt(sq[:1, :1]) + 1e-07)
    for p in range(NP):
        arrived(ghr.at[p], ("gh", p))
        val = (gbuf[p, hi, xx] + ghr[p].astype(F32)) * factor * factor * 768.0
        gram_out[:, p * width : (p + 1) * width] = val

    for copy in started:
        copy.wait_send()


def body(inputs, out_grad, w_in, w_out):
    vmem = pl.BlockSpec(memory_space=pltpu.VMEM)
    hbm = pl.BlockSpec(memory_space=pl.ANY)
    dma = pltpu.SemaphoreType.DMA
    n = len(ORDER)
    width = 768 // NP
    dx_t, weight_grad, gram = pl.pallas_call(
        kernel,
        out_shape=(
            jax.ShapeDtypeStruct((96, 256), BF),
            jax.ShapeDtypeStruct((768, 256), BF),
            jax.ShapeDtypeStruct((96, 768), F32),
        ),
        in_specs=[hbm] * 4,
        out_specs=(vmem,) * 3,
        scratch_shapes=[
            pltpu.VMEM((2, 256, 96), BF),
            pltpu.VMEM((2, 2, 768, 256), BF),
            pltpu.VMEM((4, 768, 256), BF),
            pltpu.VMEM((4, 256, 768), BF),
            pltpu.VMEM((n, 2, CH, 256), BF),
            pltpu.VMEM((n, 2, CH, 256), F32),
            pltpu.VMEM((n, 2, CH // 2, 256), BF),
            pltpu.VMEM((n, 2, CH // 2, 256), BF),
            pltpu.VMEM((n, 2, CH // 4, 256), BF),
            pltpu.VMEM((n, 2, CH // 4, 256), BF),
            pltpu.VMEM((n, 2, CH // 8, 256), BF),
            pltpu.VMEM((n, CH, 256), BF),
            pltpu.VMEM((2, 768, 256), F32),
            pltpu.VMEM((2, 768, 256), BF),
            pltpu.VMEM((2, 7, 96, 256), BF),
            pltpu.VMEM((96, 256), BF),
            pltpu.VMEM((96, 256), BF),
            pltpu.VMEM((NH, 2, 384, CH), F32),
            pltpu.VMEM((NH, 768, CH), F32),
            pltpu.VMEM((NH, 6, 384, CH), BF),
            pltpu.VMEM((NH, 6, 384, CH), BF),
            pltpu.VMEM((NP, 2, 4, 96, width), F32),
            pltpu.VMEM((NP, 6, 96, width), BF),
            pltpu.VMEM((NP, 6, 96, width), BF),
            pltpu.VMEM((NP, 96, width), BF),
            pltpu.VMEM((NP, 96, width), BF),
            pltpu.VMEM((8, 128), F32),
            pltpu.VMEM((7, 8, 128), F32),
            dma((4,)), dma((SLOTS,)), dma((SLOTS,)),
        ],
        compiler_params=pltpu.CompilerParams(
            collective_id=0, has_side_effects=True, vmem_limit_bytes=48 * 1024 * 1024
        ),
        cost_estimate=pl.CostEstimate(
            flops=3_600_000_000, bytes_accessed=4_000_000, transcendentals=131072
        ),
    )(inputs, out_grad, w_in, w_out)
    return (dx_t.T, weight_grad, gram[None])


def solution(mesh):
    placed = (
        P("gx", ("gy", "gz")),
        P("gx", ("gy", "gz")),
        P("gy", ("gx", "gz")),
        P(("gx", "gz"), "gy"),
    )
    return jax.shard_map(
        body,
        mesh=mesh,
        in_specs=placed,
        out_specs=(P("gx", ("gy", "gz")), P("gy", ("gx", "gz")), P("gz", ("gy", "gx"), None)),
        check_vma=False,
    )
```

```python
import jax
import jax.numpy as jnp
from jax import lax
from jax.experimental import pallas as pl
from jax.experimental.pallas import tpu as pltpu
from jax.sharding import PartitionSpec as P

GELU_COEF = 0.7978845608
BF = jnp.bfloat16
F32 = jnp.float32
MESH = pl.DeviceIdType.MESH
UP = float(2.0**30)
DOWN = float(2.0**-30)
NH = 2
CH = 256 // NH
NP = 3
KINDS = 16
SLOTS = 160
TOGETHER = {"ah": 2, "dx": 2, "sq": 1}

SCHEDULE = [
    ("start",), ("wstart", 0), ("z", 0, 1, 1, 1), ("z", 0, 0, 0, 1), ("wstart", 1), ("z", 0, 1, 0, 1), ("hs", 0),
    ("z", 0, 0, 1, 1), ("z", 0, 1, 1, 2), ("z", 0, 0, 0, 2), ("hs", 1), ("z", 0, 0, 1, 2), ("z", 1, 0, 0, 1),
    ("z", 0, 0, 0, 3), ("z", 0, 1, 0, 2), ("z", 0, 1, 1, 3), ("z", 1, 1, 1, 1), ("wf", 0, 0), ("z", 1, 0, 1, 1),
    ("z", 1, 0, 0, 2), ("z", 0, 0, 0, 4), ("z", 0, 0, 1, 3), ("wf", 0, 1), ("z", 1, 1, 1, 2), ("z", 0, 1, 0, 3),
    ("z", 0, 1, 1, 4), ("A", 3, 0, 0), ("z", 1, 1, 0, 1), ("A", 1, 0, 0), ("z", 1, 0, 1, 2), ("B", 3, 0, 0),
    ("z", 1, 0, 0, 3), ("B", 1, 0, 0), ("wf", 1, 0), ("A", 0, 1, 0), ("A", 3, 1, 0), ("wf", 1, 1), ("z", 1, 1, 1, 3),
    ("z", 1, 1, 0, 2), ("B", 3, 1, 0), ("z", 1, 0, 0, 4), ("A", 1, 1, 0), ("A", 0, 0, 0), ("z", 1, 0, 1, 3),
    ("B2", 3, 0, 0), ("B", 1, 1, 0), ("B", 0, 1, 0), ("B2", 1, 0, 0), ("z", 1, 1, 1, 4), ("A", 2, 0, 0),
    ("B2", 3, 1, 0), ("z", 1, 1, 0, 3), ("A", 1, 0, 1), ("B", 2, 0, 0), ("A", 2, 0, 1), ("B", 1, 0, 1),
    ("A", 3, 0, 1), ("B", 2, 0, 1), ("B", 3, 0, 1), ("B2", 1, 1, 0), ("A", 3, 1, 1), ("C", 3, 0, 0), ("A", 2, 1, 1),
    ("B2", 2, 0, 0), ("A", 2, 1, 0), ("C", 1, 0, 0), ("A", 1, 1, 1), ("B", 2, 1, 1), ("B2", 2, 0, 1), ("B", 2, 1, 0),
    ("B2", 3, 0, 1), ("A", 0, 0, 1), ("A", 0, 1, 1), ("B", 1, 1, 1), ("B2", 1, 0, 1), ("B", 3, 1, 1), ("C", 2, 0, 0),
    ("B2", 2, 1, 1), ("D", 3, 0, 0), ("C", 2, 0, 1), ("B2", 2, 1, 0), ("C", 3, 0, 1), ("C", 1, 0, 1), ("B", 0, 0, 1),
    ("B", 0, 1, 1), ("B2", 3, 1, 1), ("C", 3, 1, 0), ("C", 2, 1, 1), ("D", 2, 0, 0), ("D", 1, 0, 0), ("D", 2, 0, 1),
    ("C", 2, 1, 0), ("E", 1, 0, 0), ("E", 2, 0, 0), ("B2", 1, 1, 1), ("B2", 0, 0, 1), ("D", 3, 0, 1), ("E", 2, 0, 1),
    ("dw", 2, 0), ("B2", 0, 1, 1), ("D", 1, 0, 1), ("C", 1, 1, 0), ("C", 3, 1, 1), ("E", 3, 0, 0), ("B2", 0, 1, 0),
    ("E", 3, 0, 1), ("E", 1, 0, 1), ("dw", 3, 0), ("B", 0, 0, 0), ("dw", 1, 0), ("C", 1, 1, 1), ("D", 2, 1, 0),
    ("D", 2, 1, 1), ("C", 0, 0, 1), ("E", 2, 1, 0), ("E", 2, 1, 1), ("dw", 2, 1), ("C", 0, 1, 1), ("D", 3, 1, 0),
    ("add", 0, 1), ("B2", 0, 0, 0), ("E", 3, 1, 0), ("add", 0, 0), ("C", 0, 1, 0), ("D", 3, 1, 1), ("D", 1, 1, 0),
    ("D", 1, 1, 1), ("E", 3, 1, 1), ("dw", 3, 1), ("E", 1, 1, 0), ("E", 1, 1, 1), ("dw", 1, 1), ("D", 0, 0, 1),
    ("C", 0, 0, 0), ("D", 0, 1, 1), ("add", 1, 1), ("add", 1, 0), ("E", 0, 0, 1), ("E", 0, 1, 1), ("dx", 1),
    ("D", 0, 1, 0), ("E", 0, 1, 0), ("dw", 0, 1), ("D", 0, 0, 0), ("E", 0, 0, 0), ("dw", 0, 0), ("own", 0),
    ("own", 1), ("sq",), ("g", 0), ("g", 2), ("g", 1), ("g2", 0), ("dx", 0), ("ga", 0, 0), ("ga", 0, 1), ("g2", 1),
    ("dxs", 1), ("ga", 1, 1), ("ga", 2, 1), ("ga", 1, 0), ("ga", 2, 0), ("go", 0), ("g2", 2), ("go", 1), ("go", 2),
    ("dxs", 0), ("gf", 0), ("gf", 1), ("dxf",), ("gf", 2),
]


def index(s, b, r):
    return (s * NH + b) * 2 + r


def gelu_slope(preact):
    inner = GELU_COEF * (preact + 0.044715 * preact * preact * preact)
    tanh_part = jnp.tanh(inner)
    return 0.5 * (1.0 + tanh_part) + 0.5 * preact * (1.0 - tanh_part * tanh_part) * GELU_COEF * (
        1.0 + 3.0 * 0.044715 * preact * preact
    )


def dot(a, b, ca, cb):
    return lax.dot_general(a, b, (((ca,), (cb,)), ((), ())), preferred_element_type=F32)


def kernel(
    x_in, g_in, win, wout, dx_out, dw_out, gram_out,
    xg, wi, wo, psend, pown, crecv, ysend, yrecv, y2send, y2recv, ht,
    dxacc, dxo, dxs, dxr, dxh, dxhr, dwf, dwf0, dws, dwr,
    gbuf, gsend, grecv, ghs, ghr, sqs, sqr, l_sem, s_all, r_all,
):
    gx = lax.axis_index("gx")
    gy = lax.axis_index("gy")
    z = lax.axis_index("gz")
    hi, xx = gx // 4, gx % 4
    yy, cc = gy // 2, gy % 2
    b0, b1 = yy % 2, yy // 2
    xp = {"gx": hi * 4 + (xx + 1) % 4}
    xm = {"gx": hi * 4 + (xx + 3) % 4}
    h_dev = {"gx": (1 - hi) * 4 + xx}
    c_dev = {"gy": yy * 2 + 1 - cc}
    y1_dev = {"gy": (b1 * 2 + 1 - b0) * 2 + cc}
    y2_dev = {"gy": ((1 - b1) * 2 + b0) * 2 + cc}
    y3_dev = {"gy": ((1 - b1) * 2 + 1 - b0) * 2 + cc}
    zp, zm = {"gz": (z + 1) % 8}, {"gz": (z + 7) % 8}

    barrier = pltpu.get_barrier_semaphore()
    partners = [{"gx": (gx + k) % 8} for k in range(1, 8)]
    partners += [{"gz": (z + k) % 8} for k in range(1, 8)]
    partners += [c_dev, y1_dev, y2_dev, y3_dev]
    for dev in partners:
        pl.semaphore_signal(barrier, inc=1, device_id=dev, device_id_type=MESH)

    slots = {}
    kinds = {}

    def rc(src, dst, name, dev):
        kind = name[0] + str(name[2] % 2) if name[0] == "w" else name[0]
        group = name[: TOGETHER[name[0]]] if name[0] in TOGETHER else name
        k = kinds.setdefault(kind, len(kinds))
        slot = slots.setdefault(group, len(slots))
        return pltpu.make_async_remote_copy(
            src_ref=src, dst_ref=dst, send_sem=s_all.at[k], recv_sem=r_all.at[slot],
            device_id=dev, device_id_type=MESH,
        )

    def send(src, dst, name, dev):
        rc(src, dst, name, dev).start()

    waited = set()

    def arrived(ref, name):
        if name not in waited:
            waited.add(name)
            rc(ref, ref, name, c_dev).wait_recv()

    def zrows(i):
        return pl.ds(pl.multiple_of(i * 96, 32), 96)

    own = zrows(z)
    local = [
        pltpu.make_async_copy(x_in, xg.at[0, 0, own, :], l_sem.at[0]),
        pltpu.make_async_copy(g_in, xg.at[1, 0, own, :], l_sem.at[1]),
        pltpu.make_async_copy(win, wi.at[0], l_sem.at[2]),
        pltpu.make_async_copy(wout, wo.at[0], l_sem.at[3]),
    ]
    for copy in local:
        copy.start()
    pl.semaphore_wait(barrier, len(partners))

    hops = ((4, 3), (3, 4))

    def zref(r, a, d, s):
        begun = (z + 8 - s) % 8 if d == 0 else (z + s) % 8
        return xg.at[a, r, zrows(begun), :]

    def zsend(r, a, d, s):
        ref = zref(r, a, d, s - 1)
        src = (x_in, g_in)[a] if r == 0 and s == 1 else ref
        send(src, ref, ("z", r, a, d, s), zp if d == 0 else zm)

    def do_z(r, a, d, s):
        arrived(zref(r, a, d, s), ("z", r, a, d, s))
        if s < hops[a][d]:
            zsend(r, a, d, s + 1)

    def do_hs(a):
        arrived(xg.at[a, 1, own, :], ("h", a))
        for d in range(2):
            zsend(1, a, d, 1)

    def do_start():
        for a in range(2):
            send((x_in, g_in)[a], xg.at[a, 1, own, :], ("h", a), h_dev)
            for d in range(2):
                zsend(0, a, d, 1)

    def piece(b):
        return pl.ds(b * CH, CH)

    def do_wstart(b):
        send(win.at[:, piece(b)], wi.at[3, :, piece(b)], ("w", b, 0), xp)
        send(win.at[:, piece(b)], wi.at[1, :, piece(b)], ("w", b, 2), xm)
        send(wout.at[piece(b), :], wo.at[3, piece(b), :], ("w", b, 1), xp)
        send(wout.at[piece(b), :], wo.at[1, piece(b), :], ("w", b, 3), xm)

    def do_wf(b, i):
        if i == 0:
            arrived(wi.at[3, :, piece(b)], ("w", b, 0))
            send(wi.at[3, :, piece(b)], wi.at[2, :, piece(b)], ("w", b, 4), xp)
        else:
            arrived(wo.at[1, piece(b), :], ("w", b, 3))
            send(wo.at[1, piece(b), :], wo.at[2, piece(b), :], ("w", b, 5), xm)

    own_w = []

    def w_here(s, b):
        if s == 1:
            arrived(wi.at[1, :, piece(b)], ("w", b, 2))
        elif s == 2:
            arrived(wi.at[2, :, piece(b)], ("w", b, 4))
            arrived(wo.at[2, piece(b), :], ("w", b, 5))
        elif s == 3:
            arrived(wo.at[3, piece(b), :], ("w", b, 1))

    def rows(i, n):
        return pl.ds(pl.multiple_of(i * n, n), n)

    def do_a(s, b, r):
        c = index(s, b, r)
        if not own_w:
            own_w.append(True)
            for copy in local:
                copy.wait()
        w_here(s, b)
        pre = dot(wi[s, :, b * CH : (b + 1) * CH], xg[0, r], 0, 0)
        back = dot(wo[s, b * CH : (b + 1) * CH, :], xg[1, r], 1, 0)
        for k, val in enumerate((pre, back)):
            pown[c, k] = val
            psend[c, k] = val.astype(BF)
        send(psend.at[c, :, rows(1 - cc, CH // 2), :], crecv.at[c], ("c", c), c_dev)

    def do_b(s, b, r):
        c = index(s, b, r)
        arrived(crecv.at[c], ("c", c))
        total = pown[c, :, rows(cc, CH // 2), :] + crecv[c].astype(F32)
        pown[c, :, : CH // 2, :] = total
        ysend[c] = total.astype(BF)
        send(ysend.at[c, :, rows(1 - b0, CH // 4), :], yrecv.at[c], ("y", c), y1_dev)

    def do_b2(s, b, r):
        c = index(s, b, r)
        arrived(yrecv.at[c], ("y", c))
        total = pown[c, :, rows(b0, CH // 4), :] + yrecv[c].astype(F32)
        pown[c, :, : CH // 4, :] = total
        y2send[c] = total.astype(BF)
        send(y2send.at[c, :, rows(1 - b1, CH // 8), :], y2recv.at[c], ("y2", c), y2_dev)

    def hrows(p0, p1):
        return rows(cc * 4 + p0 * 2 + p1, CH // 8)

    def do_c(s, b, r):
        c = index(s, b, r)
        arrived(y2recv.at[c], ("y2", c))
        total = pown[c, :, rows(b1, CH // 8), :] + y2recv[c].astype(F32)
        ht[c, hrows(b0, b1), :] = (total[1] * gelu_slope(total[0])).astype(BF)
        ref = ht.at[c, hrows(b0, b1), :]
        for k, dev in ((1, y1_dev), (2, y2_dev), (3, y3_dev)):
            send(ref, ref, ("ah", c, k), dev)

    def do_d(s, b, r):
        c = index(s, b, r)
        arrived(ht.at[c, : 3 * CH // 8, :], ("ah", c))
        ref = ht.at[c, rows(cc, CH // 2), :]
        send(ref, ref, ("ac", c), c_dev)

    first = [True, True]

    def do_e(s, b, r):
        c = index(s, b, r)
        arrived(ht.at[c, rows(1 - cc, CH // 2), :], ("ac", c))
        val = dot(wi[s, :, b * CH : (b + 1) * CH], ht[c], 1, 0)
        dxacc[r] = val if first[r] else dxacc[r] + val
        first[r] = False

    def do_dx(r):
        dxs[r] = dxacc[r].astype(BF)
        for k in (4, 3, 5, 2, 6, 1, 7):
            to = (z + k) % 8
            send(dxs.at[r, zrows(to), :], dxr.at[r, k - 1], ("dx", r, k), {"gz": to})

    def do_dw(s, b):
        dw = dot(xg[0, 0], ht[index(s, b, 0)], 1, 1) + dot(xg[0, 1], ht[index(s, b, 1)], 1, 1)
        if s == 0:
            dwf0[b] = dw
        elif s == 1:
            dwf[b, 0] = dw[:384]
            put_dw(b, 2, dw[384:], xp)
        elif s == 2:
            put_dw(b, 0, dw[:384], xp)
            put_dw(b, 1, dw[384:], xm)
        else:
            dwf[b, 1] = dw[384:]
            put_dw(b, 3, dw[:384], xm)

    def put_dw(b, i, val, dev):
        dws[b, i] = val.astype(BF)
        send(dws.at[b, i], dwr.at[b, i], ("dw", b, i), dev)

    def do_add(b, i):
        arrived(dwr.at[b, i], ("dw", b, i))
        put_dw(b, 4 + i, dwf[b, i] + dwr[b, i].astype(F32), xm if i else xp)

    def do_own(b):
        for i in (2, 3, 4, 5):
            arrived(dwr.at[b, i], ("dw", b, i))
        low = dwf0[b, :384] + dwr[b, 3].astype(F32) + dwr[b, 4].astype(F32)
        high = dwf0[b, 384:] + dwr[b, 2].astype(F32) + dwr[b, 5].astype(F32)
        dw_out[:384, b * CH : (b + 1) * CH] = low.astype(BF)
        dw_out[384:, b * CH : (b + 1) * CH] = high.astype(BF)

    scaled = {}

    def do_sq():
        wf = dw_out[...].astype(F32)
        sqs[...] = jnp.broadcast_to(jnp.sum(wf * wf), (8, 128))
        for k in range(1, 8):
            send(sqs, sqr.at[k - 1], ("sq", k), {"gx": (gx + k) % 8})
        scaled["w"] = (wf * UP).astype(BF)

    x1, x2, x3 = (xx + 1) % 4, (xx + 2) % 4, (xx + 3) % 4
    width = 768 // NP

    def put_g(p, i, val, dev):
        gsend[p, i] = val.astype(BF)
        send(gsend.at[p, i], grecv.at[p, i], ("g", p, i), dev)

    def do_g(p):
        ws = scaled["w"]
        gbuf[p] = dot(ws, ws[p * width : (p + 1) * width], 1, 1).reshape(2, 4, 96, width)
        put_g(p, 0, gbuf[p, 0, x2], xp)
        put_g(p, 1, gbuf[p, 1, x2], xm)

    def do_g2(p):
        put_g(p, 2, gbuf[p, 1, x1], xp)
        put_g(p, 3, gbuf[p, 0, x3], xm)

    def do_ga(p, i):
        arrived(grecv.at[p, i], ("g", p, i))
        mine = gbuf[p, 1, x3] if i else gbuf[p, 0, x1]
        put_g(p, 4 + i, mine + grecv[p, i].astype(F32), xm if i else xp)

    def do_go(p):
        for i in (2, 3, 4, 5):
            arrived(grecv.at[p, i], ("g", p, i))
        gbuf[p, 0, xx] = gbuf[p, 0, xx] + grecv[p, 3].astype(F32) + grecv[p, 4].astype(F32)
        gbuf[p, 1, xx] = gbuf[p, 1, xx] + grecv[p, 2].astype(F32) + grecv[p, 5].astype(F32)
        ghs[p] = gbuf[p, 1 - hi, xx].astype(BF)
        send(ghs.at[p], ghr.at[p], ("gh", p), h_dev)

    def do_gf(p):
        if "factor" not in scaled:
            sq = sqs[...]
            arrived(sqr, ("sq",))
            for k in range(1, 8):
                sq = sq + sqr[k - 1]
            scaled["factor"] = DOWN / (jnp.sqrt(sq[:1, :1]) + 1e-07)
        factor = scaled["factor"]
        arrived(ghr.at[p], ("gh", p))
        val = (gbuf[p, hi, xx] + ghr[p].astype(F32)) * factor * factor * 768.0
        gram_out[:, p * width : (p + 1) * width] = val

    def do_dxs(r):
        total = dxacc[r, own, :]
        arrived(dxr.at[r], ("dx", r))
        for k in range(1, 8):
            total = total + dxr[r, k - 1].astype(F32)
        if r == 1:
            dxh[...] = total.astype(BF)
            send(dxh, dxhr, ("dxh",), h_dev)
        else:
            dxo[...] = total

    def do_dxf():
        arrived(dxhr, ("dxh",))
        dx_out[...] = (dxo[...] + dxhr[...].astype(F32)).astype(BF)

    steps = {
        "start": do_start, "wstart": do_wstart, "hs": do_hs, "z": do_z, "wf": do_wf,
        "A": do_a, "B": do_b, "B2": do_b2, "C": do_c, "D": do_d, "E": do_e, "dw": do_dw, "add": do_add, "own": do_own,
        "sq": do_sq, "g": do_g, "g2": do_g2, "ga": do_ga, "go": do_go, "gf": do_gf,
        "dx": do_dx, "dxs": do_dxs, "dxf": do_dxf,
    }
    for step in SCHEDULE:
        steps[step[0]](*step[1:])

    totals = {
        "h": xg.at[:, 0, :96, :], "z": xg.at[:, :, :672, :], "w0": wi.at[:3], "w1": wo.at[:3],
        "c": crecv, "y": yrecv, "y2": y2recv, "ah": ht.at[:, : 3 * CH // 8, :], "ac": ht.at[:, : CH // 2, :],
        "dw": dwr, "dx": dxr, "sq": sqr, "g": grecv, "gh": ghr, "dxh": dxhr,
    }
    for kind, ref in totals.items():
        k = kinds[kind]
        pltpu.make_async_remote_copy(
            src_ref=ref, dst_ref=ref, send_sem=s_all.at[k], recv_sem=r_all.at[0],
            device_id=c_dev, device_id_type=MESH,
        ).wait_send()


def body(inputs, out_grad, w_in, w_out):
    vmem = pl.BlockSpec(memory_space=pltpu.VMEM)
    hbm = pl.BlockSpec(memory_space=pl.ANY)
    dma = pltpu.SemaphoreType.DMA
    n = 8 * NH
    width = 768 // NP
    dx_t, weight_grad, gram = pl.pallas_call(
        kernel,
        out_shape=(
            jax.ShapeDtypeStruct((96, 256), BF),
            jax.ShapeDtypeStruct((768, 256), BF),
            jax.ShapeDtypeStruct((96, 768), F32),
        ),
        in_specs=[hbm] * 4,
        out_specs=(vmem,) * 3,
        scratch_shapes=[
            pltpu.VMEM((2, 2, 768, 256), BF),
            pltpu.VMEM((4, 768, 256), BF),
            pltpu.VMEM((4, 256, 768), BF),
            pltpu.VMEM((n, 2, CH, 256), BF),
            pltpu.VMEM((n, 2, CH, 256), F32),
            pltpu.VMEM((n, 2, CH // 2, 256), BF),
            pltpu.VMEM((n, 2, CH // 2, 256), BF),
            pltpu.VMEM((n, 2, CH // 4, 256), BF),
            pltpu.VMEM((n, 2, CH // 4, 256), BF),
            pltpu.VMEM((n, 2, CH // 8, 256), BF),
            pltpu.VMEM((n, CH, 256), BF),
            pltpu.VMEM((2, 768, 256), F32),
            pltpu.VMEM((96, 256), F32),
            pltpu.VMEM((2, 768, 256), BF),
            pltpu.VMEM((2, 7, 96, 256), BF),
            pltpu.VMEM((96, 256), BF),
            pltpu.VMEM((96, 256), BF),
            pltpu.VMEM((NH, 2, 384, CH), F32),
            pltpu.VMEM((NH, 768, CH), F32),
            pltpu.VMEM((NH, 6, 384, CH), BF),
            pltpu.VMEM((NH, 6, 384, CH), BF),
            pltpu.VMEM((NP, 2, 4, 96, width), F32),
            pltpu.VMEM((NP, 6, 96, width), BF),
            pltpu.VMEM((NP, 6, 96, width), BF),
            pltpu.VMEM((NP, 96, width), BF),
            pltpu.VMEM((NP, 96, width), BF),
            pltpu.VMEM((8, 128), F32),
            pltpu.VMEM((7, 8, 128), F32),
            dma((4,)), dma((KINDS,)), dma((SLOTS,)),
        ],
        compiler_params=pltpu.CompilerParams(
            collective_id=0, has_side_effects=True, vmem_limit_bytes=60 * 1024 * 1024
        ),
        cost_estimate=pl.CostEstimate(
            flops=3_600_000_000, bytes_accessed=4_000_000, transcendentals=131072
        ),
    )(inputs.T, out_grad.T, w_in, w_out)
    return (dx_t.T, weight_grad, gram[None])


def solution(mesh):
    placed = (
        P("gx", ("gy", "gz")),
        P("gx", ("gy", "gz")),
        P("gy", ("gx", "gz")),
        P(("gx", "gz"), "gy"),
    )
    return jax.shard_map(
        body,
        mesh=mesh,
        in_specs=placed,
        out_specs=(P("gx", ("gy", "gz")), P("gy", ("gx", "gz")), P("gz", ("gy", "gx"), None)),
        check_vma=False,
    )
```

```python
import jax
import jax.numpy as jnp
from jax import lax
from jax.experimental import pallas as pl
from jax.experimental.pallas import tpu as pltpu
from jax.sharding import PartitionSpec as P

GELU_COEF = 0.7978845608
BF = jnp.bfloat16
F32 = jnp.float32
MESH = pl.DeviceIdType.MESH
UP = float(2.0**30)
DOWN = float(2.0**-30)
NH = 2
CH = 256 // NH
NP = 6
KINDS = 16
ZT = 1
SLOTS = 156
TOGETHER = {"ah": 2, "dx": 2, "sq": 1}
LATE = (2, 3, 4, 5)

SCHEDULE = [
    ("start",), ("wstart", 0), ("z", 0, 0, 0, 1, 0), ("wstart", 1), ("z", 0, 0, 1, 1, 0), ("z", 0, 1, 0, 1, 0),
    ("z", 0, 1, 1, 1, 0), ("hs", 0, 0), ("z", 0, 0, 0, 2, 0), ("hs", 1, 0), ("z", 0, 1, 1, 2, 0),
    ("z", 0, 0, 1, 2, 0), ("z", 1, 0, 0, 1, 0), ("z", 0, 0, 0, 3, 0), ("z", 1, 1, 1, 1, 0), ("z", 0, 1, 0, 2, 0),
    ("z", 1, 1, 0, 1, 0), ("wf", 0, 0), ("z", 0, 1, 1, 3, 0), ("z", 1, 0, 0, 2, 0), ("z", 1, 0, 1, 1, 0),
    ("z", 0, 0, 0, 4, 0), ("wf", 1, 0), ("z", 1, 1, 1, 2, 0), ("z", 0, 1, 0, 3, 0), ("z", 0, 0, 1, 3, 0),
    ("wf", 0, 1), ("z", 0, 1, 1, 4, 0), ("A", 1, 0, 0), ("A", 3, 0, 0), ("A", 0, 1, 0), ("B", 1, 0, 0),
    ("z", 1, 0, 1, 2, 0), ("z", 1, 1, 0, 2, 0), ("B", 3, 0, 0), ("z", 1, 0, 0, 3, 0), ("B", 0, 1, 0), ("wf", 1, 1),
    ("A", 1, 1, 0), ("z", 1, 1, 1, 3, 0), ("A", 3, 1, 0), ("B", 1, 1, 0), ("B2", 3, 0, 0), ("z", 1, 0, 1, 3, 0),
    ("B2", 1, 0, 0), ("B", 3, 1, 0), ("B2", 0, 1, 0), ("z", 1, 0, 0, 4, 0), ("A", 2, 0, 0), ("z", 1, 1, 0, 3, 0),
    ("z", 1, 1, 1, 4, 0), ("A", 2, 0, 1), ("B2", 1, 1, 0), ("B", 2, 0, 0), ("A", 3, 0, 1), ("B", 2, 0, 1),
    ("A", 1, 0, 1), ("B", 3, 0, 1), ("A", 1, 1, 1), ("B2", 3, 1, 0), ("B", 1, 0, 1), ("C", 3, 0, 0), ("A", 0, 1, 1),
    ("A", 2, 1, 0), ("B2", 2, 0, 0), ("A", 2, 1, 1), ("B2", 2, 0, 1), ("B", 2, 1, 0), ("A", 0, 0, 1), ("B", 2, 1, 1),
    ("B2", 3, 0, 1), ("B2", 1, 0, 1), ("B", 1, 1, 1), ("A", 3, 1, 1), ("C", 1, 0, 0), ("C", 2, 0, 0), ("B", 3, 1, 1),
    ("B2", 2, 1, 0), ("B2", 2, 1, 1), ("C", 2, 0, 1), ("C", 3, 0, 1), ("B", 0, 1, 1), ("D", 3, 0, 0), ("B", 0, 0, 1),
    ("C", 1, 0, 1), ("B2", 1, 1, 1), ("A", 0, 0, 0), ("B2", 3, 1, 1), ("E", 3, 0, 0), ("C", 2, 1, 0), ("D", 1, 0, 0),
    ("D", 2, 0, 0), ("C", 2, 1, 1), ("E", 1, 0, 0), ("B2", 0, 1, 1), ("D", 2, 0, 1), ("E", 2, 0, 0), ("B2", 0, 0, 1),
    ("C", 1, 1, 0), ("D", 3, 0, 1), ("E", 2, 0, 1), ("dw", 2, 0), ("B", 0, 0, 0), ("C", 3, 1, 0), ("E", 3, 0, 1),
    ("D", 1, 0, 1), ("C", 3, 1, 1), ("C", 1, 1, 1), ("dw", 3, 0), ("E", 1, 0, 1), ("dw", 1, 0), ("D", 2, 1, 1),
    ("C", 0, 1, 1), ("D", 2, 1, 0), ("C", 0, 0, 1), ("E", 2, 1, 1), ("B2", 0, 0, 0), ("E", 2, 1, 0), ("dw", 2, 1),
    ("C", 0, 1, 0), ("D", 1, 1, 0), ("add", 0, 1), ("D", 3, 1, 0), ("D", 3, 1, 1), ("add", 0, 0), ("D", 1, 1, 1),
    ("E", 1, 1, 0), ("E", 3, 1, 0), ("E", 3, 1, 1), ("D", 0, 1, 1), ("dw", 3, 1), ("E", 1, 1, 1), ("D", 0, 0, 1),
    ("dw", 1, 1), ("C", 0, 0, 0), ("E", 0, 1, 1), ("E", 0, 0, 1), ("dx", 1), ("D", 0, 1, 0), ("add", 1, 0),
    ("add", 1, 1), ("E", 0, 1, 0), ("dw", 0, 1), ("D", 0, 0, 0), ("E", 0, 0, 0), ("dw", 0, 0), ("own", 0), ("own", 1),
    ("sq",), ("g", 5), ("g", 0), ("g", 1), ("g", 3), ("sq2",), ("g2", 5), ("g", 4), ("dx", 0), ("g", 2), ("ga", 5, 0),
    ("ga", 5, 1), ("g2", 0), ("ga", 0, 0), ("ga", 0, 1), ("ga", 1, 1), ("g2", 1), ("dxs", 1), ("ga", 1, 0),
    ("ga", 4, 0), ("g2", 4), ("ga", 4, 1), ("ga", 3, 0), ("ga", 3, 1), ("go", 5), ("g2", 3), ("ga", 2, 0),
    ("ga", 2, 1), ("go", 0), ("g2", 2), ("go", 1), ("go", 4), ("go", 3), ("go", 2), ("gf", 0), ("gf", 5), ("gf", 1),
    ("gf", 4), ("gf", 3), ("dxs", 0), ("dxf",), ("gf", 2),
]


def index(s, b, r):
    return (s * NH + b) * 2 + r


def gelu_slope(preact):
    inner = GELU_COEF * (preact + 0.044715 * preact * preact * preact)
    tanh_part = jnp.tanh(inner)
    return 0.5 * (1.0 + tanh_part) + 0.5 * preact * (1.0 - tanh_part * tanh_part) * GELU_COEF * (
        1.0 + 3.0 * 0.044715 * preact * preact
    )


def dot(a, b, ca, cb):
    return lax.dot_general(a, b, (((ca,), (cb,)), ((), ())), preferred_element_type=F32)


def kernel(
    x_in, g_in, win, wout, dx_out, dw_out, gram_out,
    xg, wi, wo, psend, pown, crecv, ysend, yrecv, y2send, y2recv, ht,
    dxacc, dxo, dxs, dxr, dxh, dxhr, dwf, dwf0, dws, dwr,
    gbuf, gsend, grecv, ghs, ghr, sqs, sqr, l_sem, s_all, r_all,
):
    gx = lax.axis_index("gx")
    gy = lax.axis_index("gy")
    z = lax.axis_index("gz")
    hi, xx = gx // 4, gx % 4
    yy, cc = gy // 2, gy % 2
    b0, b1 = yy % 2, yy // 2
    xp = {"gx": hi * 4 + (xx + 1) % 4}
    xm = {"gx": hi * 4 + (xx + 3) % 4}
    h_dev = {"gx": (1 - hi) * 4 + xx}
    c_dev = {"gy": yy * 2 + 1 - cc}
    y1_dev = {"gy": (b1 * 2 + 1 - b0) * 2 + cc}
    y2_dev = {"gy": ((1 - b1) * 2 + b0) * 2 + cc}
    y3_dev = {"gy": ((1 - b1) * 2 + 1 - b0) * 2 + cc}
    zp, zm = {"gz": (z + 1) % 8}, {"gz": (z + 7) % 8}

    barrier = pltpu.get_barrier_semaphore()
    partners = [{"gx": (gx + k) % 8} for k in range(1, 8)]
    partners += [{"gz": (z + k) % 8} for k in range(1, 8)]
    partners += [c_dev, y1_dev, y2_dev, y3_dev]
    for dev in partners:
        pl.semaphore_signal(barrier, inc=1, device_id=dev, device_id_type=MESH)

    slots = {}
    kinds = {}

    def rc(src, dst, name, dev):
        kind = name[0] + str(name[2] % 2) if name[0] == "w" else name[0]
        group = name[: TOGETHER[name[0]]] if name[0] in TOGETHER else name
        if name[0] in ("dw", "g") and name[2] in LATE:
            group = name[:2]
        k = kinds.setdefault(kind, len(kinds))
        slot = slots.setdefault(group, len(slots))
        return pltpu.make_async_remote_copy(
            src_ref=src, dst_ref=dst, send_sem=s_all.at[k], recv_sem=r_all.at[slot],
            device_id=dev, device_id_type=MESH,
        )

    def send(src, dst, name, dev):
        rc(src, dst, name, dev).start()

    waited = set()

    def arrived(ref, name):
        if name not in waited:
            waited.add(name)
            rc(ref, ref, name, c_dev).wait_recv()

    def zrows(i):
        return pl.ds(pl.multiple_of(i * 96, 32), 96)

    own = zrows(z)
    local = [
        pltpu.make_async_copy(x_in, xg.at[0, 0, own, :], l_sem.at[0]),
        pltpu.make_async_copy(g_in, xg.at[1, 0, own, :], l_sem.at[1]),
        pltpu.make_async_copy(win, wi.at[0], l_sem.at[2]),
        pltpu.make_async_copy(wout, wo.at[0], l_sem.at[3]),
    ]
    for copy in local:
        copy.start()
    pl.semaphore_wait(barrier, len(partners))

    hops = ((4, 3), (3, 4))

    def lanes(t):
        return pl.ds(t * (256 // ZT), 256 // ZT)

    def zref(r, a, d, s, t):
        begun = (z + 8 - s) % 8 if d == 0 else (z + s) % 8
        return xg.at[a, r, zrows(begun), lanes(t)]

    def zsend(r, a, d, s, t):
        ref = zref(r, a, d, s - 1, t)
        src = (x_in, g_in)[a].at[:, lanes(t)] if r == 0 and s == 1 else ref
        send(src, ref, ("z", r, a, d, s, t), zp if d == 0 else zm)

    def do_z(r, a, d, s, t):
        arrived(zref(r, a, d, s, t), ("z", r, a, d, s, t))
        if s < hops[a][d]:
            zsend(r, a, d, s + 1, t)

    def do_hs(a, t):
        arrived(xg.at[a, 1, own, lanes(t)], ("h", a, t))
        for d in range(2):
            zsend(1, a, d, 1, t)

    def do_start():
        for a in range(2):
            for t in range(ZT):
                send((x_in, g_in)[a].at[:, lanes(t)], xg.at[a, 1, own, lanes(t)], ("h", a, t), h_dev)
        for a in range(2):
            for t in range(ZT):
                for d in range(2):
                    zsend(0, a, d, 1, t)

    def piece(b):
        return pl.ds(b * CH, CH)

    def do_wstart(b):
        send(win.at[:, piece(b)], wi.at[3, :, piece(b)], ("w", b, 0), xp)
        send(win.at[:, piece(b)], wi.at[1, :, piece(b)], ("w", b, 2), xm)
        send(wout.at[piece(b), :], wo.at[3, piece(b), :], ("w", b, 1), xp)
        send(wout.at[piece(b), :], wo.at[1, piece(b), :], ("w", b, 3), xm)

    def do_wf(b, i):
        if i == 0:
            arrived(wi.at[3, :, piece(b)], ("w", b, 0))
            send(wi.at[3, :, piece(b)], wi.at[2, :, piece(b)], ("w", b, 4), xp)
        else:
            arrived(wo.at[1, piece(b), :], ("w", b, 3))
            send(wo.at[1, piece(b), :], wo.at[2, piece(b), :], ("w", b, 5), xm)

    own_w = []

    def w_here(s, b):
        if s == 1:
            arrived(wi.at[1, :, piece(b)], ("w", b, 2))
        elif s == 2:
            arrived(wi.at[2, :, piece(b)], ("w", b, 4))
            arrived(wo.at[2, piece(b), :], ("w", b, 5))
        elif s == 3:
            arrived(wo.at[3, piece(b), :], ("w", b, 1))

    def rows(i, n):
        return pl.ds(pl.multiple_of(i * n, n), n)

    def do_a(s, b, r):
        c = index(s, b, r)
        if not own_w:
            own_w.append(True)
            for copy in local:
                copy.wait()
        w_here(s, b)
        pre = dot(wi[s, :, b * CH : (b + 1) * CH], xg[0, r], 0, 0)
        back = dot(wo[s, b * CH : (b + 1) * CH, :], xg[1, r], 1, 0)
        for k, val in enumerate((pre, back)):
            pown[c, k] = val
            psend[c, k] = val.astype(BF)
        send(psend.at[c, :, rows(1 - cc, CH // 2), :], crecv.at[c], ("c", c), c_dev)

    def do_b(s, b, r):
        c = index(s, b, r)
        arrived(crecv.at[c], ("c", c))
        total = pown[c, :, rows(cc, CH // 2), :] + crecv[c].astype(F32)
        pown[c, :, : CH // 2, :] = total
        ysend[c] = total.astype(BF)
        send(ysend.at[c, :, rows(1 - b0, CH // 4), :], yrecv.at[c], ("y", c), y1_dev)

    def do_b2(s, b, r):
        c = index(s, b, r)
        arrived(yrecv.at[c], ("y", c))
        total = pown[c, :, rows(b0, CH // 4), :] + yrecv[c].astype(F32)
        pown[c, :, : CH // 4, :] = total
        y2send[c] = total.astype(BF)
        send(y2send.at[c, :, rows(1 - b1, CH // 8), :], y2recv.at[c], ("y2", c), y2_dev)

    def hrows(p0, p1):
        return rows(cc * 4 + p0 * 2 + p1, CH // 8)

    def do_c(s, b, r):
        c = index(s, b, r)
        arrived(y2recv.at[c], ("y2", c))
        total = pown[c, :, rows(b1, CH // 8), :] + y2recv[c].astype(F32)
        ht[c, hrows(b0, b1), :] = (total[1] * gelu_slope(total[0])).astype(BF)
        ref = ht.at[c, hrows(b0, b1), :]
        for k, dev in ((1, y1_dev), (2, y2_dev), (3, y3_dev)):
            send(ref, ref, ("ah", c, k), dev)

    def do_d(s, b, r):
        c = index(s, b, r)
        arrived(ht.at[c, : 3 * CH // 8, :], ("ah", c))
        ref = ht.at[c, rows(cc, CH // 2), :]
        send(ref, ref, ("ac", c), c_dev)

    first = [True, True]

    def do_e(s, b, r):
        c = index(s, b, r)
        arrived(ht.at[c, rows(1 - cc, CH // 2), :], ("ac", c))
        val = dot(wi[s, :, b * CH : (b + 1) * CH], ht[c], 1, 0)
        dxacc[r] = val if first[r] else dxacc[r] + val
        first[r] = False

    def do_dx(r):
        dxs[r] = dxacc[r].astype(BF)
        for k in (4, 3, 5, 2, 6, 1, 7):
            to = (z + k) % 8
            send(dxs.at[r, zrows(to), :], dxr.at[r, k - 1], ("dx", r, k), {"gz": to})

    def do_dw(s, b):
        dw = dot(xg[0, 0], ht[index(s, b, 0)], 1, 1) + dot(xg[0, 1], ht[index(s, b, 1)], 1, 1)
        if s == 0:
            dwf0[b] = dw
        elif s == 1:
            dwf[b, 0] = dw[:384]
            put_dw(b, 2, dw[384:], xp)
        elif s == 2:
            put_dw(b, 0, dw[:384], xp)
            put_dw(b, 1, dw[384:], xm)
        else:
            dwf[b, 1] = dw[384:]
            put_dw(b, 3, dw[:384], xm)

    def put_dw(b, i, val, dev):
        dws[b, i] = val.astype(BF)
        send(dws.at[b, i], dwr.at[b, i], ("dw", b, i), dev)

    def do_add(b, i):
        arrived(dwr.at[b, i], ("dw", b, i))
        put_dw(b, 4 + i, dwf[b, i] + dwr[b, i].astype(F32), xm if i else xp)

    def do_own(b):
        arrived(dwr.at[b, 2:], ("dw", b, 2))
        low = dwf0[b, :384] + dwr[b, 3].astype(F32) + dwr[b, 4].astype(F32)
        high = dwf0[b, 384:] + dwr[b, 2].astype(F32) + dwr[b, 5].astype(F32)
        dw_out[:384, b * CH : (b + 1) * CH] = low.astype(BF)
        dw_out[384:, b * CH : (b + 1) * CH] = high.astype(BF)

    scaled = {}

    def do_sq():
        scaled["w"] = (dw_out[...].astype(F32) * UP).astype(BF)

    def do_sq2():
        wf = dw_out[...].astype(F32)
        sqs[...] = jnp.broadcast_to(jnp.sum(wf * wf), (8, 128))
        for k in range(1, 8):
            send(sqs, sqr.at[k - 1], ("sq", k), {"gx": (gx + k) % 8})

    x1, x2, x3 = (xx + 1) % 4, (xx + 2) % 4, (xx + 3) % 4
    width = 768 // NP

    def put_g(p, i, val, dev):
        gsend[p, i] = val.astype(BF)
        send(gsend.at[p, i], grecv.at[p, i], ("g", p, i), dev)

    def do_g(p):
        ws = scaled["w"]
        gbuf[p] = dot(ws, ws[p * width : (p + 1) * width], 1, 1).reshape(2, 4, 96, width)
        put_g(p, 0, gbuf[p, 0, x2], xp)
        put_g(p, 1, gbuf[p, 1, x2], xm)

    def do_g2(p):
        put_g(p, 2, gbuf[p, 1, x1], xp)
        put_g(p, 3, gbuf[p, 0, x3], xm)

    def do_ga(p, i):
        arrived(grecv.at[p, i], ("g", p, i))
        mine = gbuf[p, 1, x3] if i else gbuf[p, 0, x1]
        put_g(p, 4 + i, mine + grecv[p, i].astype(F32), xm if i else xp)

    def do_go(p):
        arrived(grecv.at[p, 2:], ("g", p, 2))
        gbuf[p, 0, xx] = gbuf[p, 0, xx] + grecv[p, 3].astype(F32) + grecv[p, 4].astype(F32)
        gbuf[p, 1, xx] = gbuf[p, 1, xx] + grecv[p, 2].astype(F32) + grecv[p, 5].astype(F32)
        ghs[p] = gbuf[p, 1 - hi, xx].astype(BF)
        send(ghs.at[p], ghr.at[p], ("gh", p), h_dev)

    def do_gf(p):
        if "factor" not in scaled:
            sq = sqs[...]
            arrived(sqr, ("sq",))
            for k in range(1, 8):
                sq = sq + sqr[k - 1]
            scaled["factor"] = DOWN / (jnp.sqrt(sq[:1, :1]) + 1e-07)
        factor = scaled["factor"]
        arrived(ghr.at[p], ("gh", p))
        val = (gbuf[p, hi, xx] + ghr[p].astype(F32)) * factor * factor * 768.0
        gram_out[:, p * width : (p + 1) * width] = val

    def do_dxs(r):
        total = dxacc[r, own, :]
        arrived(dxr.at[r], ("dx", r))
        for k in range(1, 8):
            total = total + dxr[r, k - 1].astype(F32)
        if r == 1:
            dxh[...] = total.astype(BF)
            send(dxh, dxhr, ("dxh",), h_dev)
        else:
            dxo[...] = total

    def do_dxf():
        arrived(dxhr, ("dxh",))
        dx_out[...] = (dxo[...] + dxhr[...].astype(F32)).astype(BF)

    steps = {
        "start": do_start, "wstart": do_wstart, "hs": do_hs, "z": do_z, "wf": do_wf,
        "A": do_a, "B": do_b, "B2": do_b2, "C": do_c, "D": do_d, "E": do_e, "dw": do_dw, "add": do_add, "own": do_own,
        "sq": do_sq, "sq2": do_sq2, "g": do_g, "g2": do_g2, "ga": do_ga, "go": do_go, "gf": do_gf,
        "dx": do_dx, "dxs": do_dxs, "dxf": do_dxf,
    }
    for step in SCHEDULE:
        steps[step[0]](*step[1:])

    totals = {
        "h": xg.at[:, 0, :96, :], "z": xg.at[:, :, :672, :], "w0": wi.at[:3], "w1": wo.at[:3],
        "c": crecv, "y": yrecv, "y2": y2recv, "ah": ht.at[:, : 3 * CH // 8, :], "ac": ht.at[:, : CH // 2, :],
        "dw": dwr, "dx": dxr, "sq": sqr, "g": grecv, "gh": ghr, "dxh": dxhr,
    }
    for kind, ref in totals.items():
        k = kinds[kind]
        pltpu.make_async_remote_copy(
            src_ref=ref, dst_ref=ref, send_sem=s_all.at[k], recv_sem=r_all.at[0],
            device_id=c_dev, device_id_type=MESH,
        ).wait_send()


def hand_on(*refs):
    sem = refs[-1]
    copies = [pltpu.make_async_copy(refs[i], refs[6 + i], sem.at[i]) for i in range(3)]
    copies += [pltpu.make_async_copy(refs[6 + i], refs[3 + i], sem.at[3 + i]) for i in range(3)]
    for copy in copies[:3]:
        copy.start()
    for i in range(3):
        copies[i].wait()
        copies[3 + i].start()
    for copy in copies[3:]:
        copy.wait()


def body(inputs, out_grad, w_in, w_out):
    vmem = pl.BlockSpec(memory_space=pltpu.VMEM)
    hbm = pl.BlockSpec(memory_space=pl.ANY)
    dma = pltpu.SemaphoreType.DMA
    n = 8 * NH
    width = 768 // NP
    out_shape = (
        jax.ShapeDtypeStruct((96, 256), BF),
        jax.ShapeDtypeStruct((768, 256), BF),
        jax.ShapeDtypeStruct((96, 768), F32),
    )
    results = pl.pallas_call(
        kernel,
        out_shape=out_shape,
        in_specs=[hbm] * 4,
        out_specs=(vmem,) * 3,
        scratch_shapes=[
            pltpu.VMEM((2, 2, 768, 256), BF),
            pltpu.VMEM((4, 768, 256), BF),
            pltpu.VMEM((4, 256, 768), BF),
            pltpu.VMEM((n, 2, CH, 256), BF),
            pltpu.VMEM((n, 2, CH, 256), F32),
            pltpu.VMEM((n, 2, CH // 2, 256), BF),
            pltpu.VMEM((n, 2, CH // 2, 256), BF),
            pltpu.VMEM((n, 2, CH // 4, 256), BF),
            pltpu.VMEM((n, 2, CH // 4, 256), BF),
            pltpu.VMEM((n, 2, CH // 8, 256), BF),
            pltpu.VMEM((n, CH, 256), BF),
            pltpu.VMEM((2, 768, 256), F32),
            pltpu.VMEM((96, 256), F32),
            pltpu.VMEM((2, 768, 256), BF),
            pltpu.VMEM((2, 7, 96, 256), BF),
            pltpu.VMEM((96, 256), BF),
            pltpu.VMEM((96, 256), BF),
            pltpu.VMEM((NH, 2, 384, CH), F32),
            pltpu.VMEM((NH, 768, CH), F32),
            pltpu.VMEM((NH, 6, 384, CH), BF),
            pltpu.VMEM((NH, 6, 384, CH), BF),
            pltpu.VMEM((NP, 2, 4, 96, width), F32),
            pltpu.VMEM((NP, 6, 96, width), BF),
            pltpu.VMEM((NP, 6, 96, width), BF),
            pltpu.VMEM((NP, 96, width), BF),
            pltpu.VMEM((NP, 96, width), BF),
            pltpu.VMEM((8, 128), F32),
            pltpu.VMEM((7, 8, 128), F32),
            dma((4,)), dma((KINDS,)), dma((SLOTS,)),
        ],
        compiler_params=pltpu.CompilerParams(
            collective_id=0, has_side_effects=True, vmem_limit_bytes=60 * 1024 * 1024
        ),
        cost_estimate=pl.CostEstimate(
            flops=3_600_000_000, bytes_accessed=4_000_000, transcendentals=131072
        ),
    )(inputs.T, out_grad.T, w_in, w_out)
    dx_t, weight_grad, gram = pl.pallas_call(
        hand_on,
        out_shape=out_shape,
        in_specs=[hbm] * 3,
        out_specs=(hbm,) * 3,
        scratch_shapes=[pltpu.VMEM(v.shape, v.dtype) for v in out_shape] + [dma((6,))],
    )(*results)
    return (dx_t.T, weight_grad, gram[None])


def solution(mesh):
    placed = (
        P("gx", ("gy", "gz")),
        P("gx", ("gy", "gz")),
        P("gy", ("gx", "gz")),
        P(("gx", "gz"), "gy"),
    )
    return jax.shard_map(
        body,
        mesh=mesh,
        in_specs=placed,
        out_specs=(P("gx", ("gy", "gz")), P("gy", ("gx", "gz")), P("gz", ("gy", "gx"), None)),
        check_vma=False,
    )
```

```python
import jax
import jax.numpy as jnp
from jax import lax
from jax.experimental import pallas as pl
from jax.experimental.pallas import tpu as pltpu
from jax.sharding import PartitionSpec as P

GELU_COEF = 0.7978845608
BF = jnp.bfloat16
F32 = jnp.float32
MESH = pl.DeviceIdType.MESH
UP = float(2.0**30)
DOWN = float(2.0**-30)
NH = 2
CH = 256 // NH
NP = 6
KINDS = 17
ZT = 2
SLOTS = 184
TOGETHER = {"ah": 2, "dx": 2, "sq": 1, "g3": 1}
LATE = (2, 3, 4, 5)

SCHEDULE = [
    ("start",), ("wstart", 0), ("z", 0, 0, 1, 1, 0), ("z", 0, 0, 0, 1, 0), ("z", 0, 1, 1, 1, 0), ("z", 0, 0, 1, 1, 1),
    ("z", 0, 0, 0, 1, 1), ("z", 0, 1, 1, 1, 1), ("z", 0, 1, 0, 1, 1), ("wstart", 1), ("z", 0, 1, 0, 1, 0),
    ("hs", 0, 0), ("hs", 0, 1), ("z", 0, 0, 0, 2, 0), ("hs", 1, 0), ("z", 0, 1, 1, 2, 0), ("z", 0, 0, 0, 2, 1),
    ("hs", 1, 1), ("z", 0, 1, 1, 2, 1), ("z", 0, 0, 1, 2, 1), ("z", 0, 0, 1, 2, 0), ("z", 1, 0, 0, 1, 0),
    ("z", 1, 0, 0, 1, 1), ("z", 0, 1, 0, 2, 0), ("z", 1, 1, 1, 1, 0), ("z", 0, 1, 0, 2, 1), ("z", 0, 1, 1, 3, 0),
    ("z", 0, 0, 0, 3, 0), ("z", 1, 1, 1, 1, 1), ("z", 0, 0, 0, 3, 1), ("wf", 0, 1), ("z", 0, 1, 1, 3, 1),
    ("z", 1, 1, 0, 1, 0), ("z", 1, 0, 1, 1, 0), ("z", 1, 0, 0, 2, 0), ("z", 1, 0, 1, 1, 1), ("z", 0, 0, 1, 3, 0),
    ("z", 1, 0, 0, 2, 1), ("z", 0, 1, 0, 3, 0), ("z", 1, 1, 0, 1, 1), ("wf", 0, 0), ("z", 1, 1, 1, 2, 0),
    ("z", 1, 1, 1, 2, 1), ("z", 0, 0, 0, 4, 1), ("z", 0, 0, 0, 4, 0), ("z", 0, 1, 1, 4, 0), ("z", 0, 0, 1, 3, 1),
    ("z", 0, 1, 1, 4, 1), ("z", 0, 1, 0, 3, 1), ("A", 3, 0, 0), ("wf", 1, 0), ("z", 1, 1, 0, 2, 0),
    ("z", 1, 0, 1, 2, 0), ("A", 1, 0, 0), ("z", 1, 0, 0, 3, 0), ("z", 1, 0, 1, 2, 1), ("B", 3, 0, 0),
    ("z", 1, 1, 0, 2, 1), ("z", 1, 0, 0, 3, 1), ("B", 1, 0, 0), ("z", 1, 1, 1, 3, 0), ("A", 0, 0, 0),
    ("z", 1, 1, 1, 3, 1), ("B", 0, 0, 0), ("A", 3, 1, 0), ("wf", 1, 1), ("A", 1, 1, 0), ("B2", 3, 0, 0),
    ("z", 1, 1, 0, 3, 0), ("z", 1, 0, 1, 3, 1), ("z", 1, 0, 1, 3, 0), ("z", 1, 0, 0, 4, 0), ("B", 3, 1, 0),
    ("z", 1, 1, 1, 4, 0), ("z", 1, 0, 0, 4, 1), ("B", 1, 1, 0), ("z", 1, 1, 0, 3, 1), ("z", 1, 1, 1, 4, 1),
    ("A", 3, 1, 1), ("A", 1, 0, 1), ("B2", 1, 0, 0), ("A", 3, 0, 1), ("B", 3, 1, 1), ("B", 1, 0, 1), ("B", 3, 0, 1),
    ("A", 2, 0, 1), ("A", 2, 0, 0), ("B2", 3, 1, 0), ("B", 2, 0, 1), ("B2", 1, 1, 0), ("B", 2, 0, 0), ("C", 3, 0, 0),
    ("B2", 3, 1, 1), ("A", 0, 1, 0), ("B2", 1, 0, 1), ("C", 1, 0, 0), ("A", 1, 1, 1), ("B2", 3, 0, 1), ("A", 2, 1, 0),
    ("A", 2, 1, 1), ("B2", 2, 0, 1), ("B", 2, 1, 0), ("B", 2, 1, 1), ("B2", 2, 0, 0), ("A", 0, 1, 1), ("C", 3, 1, 0),
    ("C", 3, 1, 1), ("D", 3, 0, 0), ("C", 1, 0, 1), ("B", 1, 1, 1), ("B2", 2, 1, 0), ("B2", 2, 1, 1), ("C", 2, 0, 1),
    ("A", 0, 0, 1), ("B", 0, 1, 1), ("C", 2, 0, 0), ("D", 1, 0, 0), ("B", 0, 0, 1), ("C", 3, 0, 1), ("D", 3, 1, 0),
    ("B2", 1, 1, 1), ("D", 3, 1, 1), ("D", 1, 0, 1), ("C", 2, 1, 0), ("E", 3, 1, 0), ("E", 1, 0, 0), ("C", 2, 1, 1),
    ("E", 3, 1, 1), ("B2", 0, 1, 1), ("E", 1, 0, 1), ("dw", 1, 0), ("dw", 3, 1), ("B2", 0, 0, 1), ("D", 2, 0, 1),
    ("B2", 0, 0, 0), ("D", 2, 0, 0), ("B", 0, 1, 0), ("C", 1, 1, 0), ("E", 2, 0, 1), ("E", 2, 0, 0), ("dw", 2, 0),
    ("C", 1, 1, 1), ("D", 2, 1, 0), ("D", 2, 1, 1), ("C", 0, 1, 1), ("E", 2, 1, 0), ("D", 3, 0, 1), ("E", 3, 0, 0),
    ("C", 0, 0, 1), ("E", 2, 1, 1), ("dw", 2, 1), ("E", 3, 0, 1), ("B2", 0, 1, 0), ("C", 0, 0, 0), ("dw", 3, 0),
    ("D", 1, 1, 0), ("add", 0, 0), ("D", 1, 1, 1), ("add", 0, 1), ("E", 1, 1, 1), ("E", 1, 1, 0), ("D", 0, 1, 1),
    ("dw", 1, 1), ("D", 0, 0, 1), ("C", 0, 1, 0), ("E", 0, 1, 1), ("E", 0, 0, 1), ("dx", 1), ("add", 1, 1),
    ("D", 0, 0, 0), ("add", 1, 0), ("D", 0, 1, 0), ("E", 0, 1, 0), ("E", 0, 0, 0), ("dw", 0, 0), ("own", 0),
    ("dw", 0, 1), ("own", 1), ("sq",), ("g", 4), ("g", 0), ("g", 5), ("g", 3), ("g2", 3), ("g", 2), ("g2", 4),
    ("dx", 0), ("g", 1), ("sq2",), ("ga", 4, 1), ("ga", 4, 0), ("ga", 5, 0), ("ga", 5, 1), ("g2", 5), ("ga", 3, 0),
    ("dxs", 1), ("ga", 3, 1), ("g2", 2), ("ga", 2, 1), ("g2", 1), ("ga", 2, 0), ("ga", 1, 1), ("go", 4), ("ga", 1, 0),
    ("go", 5), ("go", 3), ("go", 2), ("go", 1), ("gx", 0), ("gf", 5), ("gf", 4), ("dxs", 0), ("gf", 2), ("gf", 3),
    ("dxf",), ("gf", 0), ("gf", 1),
]


def index(s, b, r):
    return (s * NH + b) * 2 + r


def gelu_slope(preact):
    inner = GELU_COEF * (preact + 0.044715 * preact * preact * preact)
    tanh_part = jnp.tanh(inner)
    return 0.5 * (1.0 + tanh_part) + 0.5 * preact * (1.0 - tanh_part * tanh_part) * GELU_COEF * (
        1.0 + 3.0 * 0.044715 * preact * preact
    )


def dot(a, b, ca, cb):
    return lax.dot_general(a, b, (((ca,), (cb,)), ((), ())), preferred_element_type=F32)


def kernel(
    x_in, g_in, win, wout, dx_out, dw_out, gram_out,
    xg, wi, wo, psend, pown, crecv, ysend, yrecv, y2send, y2recv, ht,
    dxacc, dxo, dxs, dxr, dxh, dxhr, dwf, dwf0, dws, dwr,
    gbuf, gsend, grecv, ghs, ghr, gys, gyr, g3s, g3r, sqs, sqr, l_sem, s_all, r_all,
):
    gx = lax.axis_index("gx")
    gy = lax.axis_index("gy")
    z = lax.axis_index("gz")
    hi, xx = gx // 4, gx % 4
    yy, cc = gy // 2, gy % 2
    b0, b1 = yy % 2, yy // 2
    xp = {"gx": hi * 4 + (xx + 1) % 4}
    xm = {"gx": hi * 4 + (xx + 3) % 4}
    h_dev = {"gx": (1 - hi) * 4 + xx}
    c_dev = {"gy": yy * 2 + 1 - cc}
    y1_dev = {"gy": (b1 * 2 + 1 - b0) * 2 + cc}
    y2_dev = {"gy": ((1 - b1) * 2 + b0) * 2 + cc}
    y3_dev = {"gy": ((1 - b1) * 2 + 1 - b0) * 2 + cc}
    zp, zm = {"gz": (z + 1) % 8}, {"gz": (z + 7) % 8}

    barrier = pltpu.get_barrier_semaphore()
    partners = [{"gx": (gx + k) % 8} for k in range(1, 8)]
    partners += [{"gz": (z + k) % 8} for k in range(1, 8)]
    partners += [c_dev, y1_dev, y2_dev, y3_dev]
    for dev in partners:
        pl.semaphore_signal(barrier, inc=1, device_id=dev, device_id_type=MESH)

    slots = {}
    kinds = {}

    def rc(src, dst, name, dev):
        kind = name[0] + str(name[2] % 2) if name[0] == "w" else name[0]
        group = name[: TOGETHER[name[0]]] if name[0] in TOGETHER else name
        if name[0] in ("dw", "g") and name[2] in LATE:
            group = name[:2]
        k = kinds.setdefault(kind, len(kinds))
        slot = slots.setdefault(group, len(slots))
        return pltpu.make_async_remote_copy(
            src_ref=src, dst_ref=dst, send_sem=s_all.at[k], recv_sem=r_all.at[slot],
            device_id=dev, device_id_type=MESH,
        )

    def send(src, dst, name, dev):
        rc(src, dst, name, dev).start()

    waited = set()

    def arrived(ref, name):
        if name not in waited:
            waited.add(name)
            rc(ref, ref, name, c_dev).wait_recv()

    def zrows(i):
        return pl.ds(pl.multiple_of(i * 96, 32), 96)

    own = zrows(z)
    local = [
        pltpu.make_async_copy(x_in, xg.at[0, 0, own, :], l_sem.at[0]),
        pltpu.make_async_copy(g_in, xg.at[1, 0, own, :], l_sem.at[1]),
        pltpu.make_async_copy(win, wi.at[0], l_sem.at[2]),
        pltpu.make_async_copy(wout, wo.at[0], l_sem.at[3]),
    ]
    for copy in local:
        copy.start()
    pl.semaphore_wait(barrier, len(partners))

    hops = ((4, 3), (3, 4))

    def lanes(t):
        return pl.ds(t * (256 // ZT), 256 // ZT)

    def zref(r, a, d, s, t):
        begun = (z + 8 - s) % 8 if d == 0 else (z + s) % 8
        return xg.at[a, r, zrows(begun), lanes(t)]

    def zsend(r, a, d, s, t):
        ref = zref(r, a, d, s - 1, t)
        src = (x_in, g_in)[a].at[:, lanes(t)] if r == 0 and s == 1 else ref
        send(src, ref, ("z", r, a, d, s, t), zp if d == 0 else zm)

    def do_z(r, a, d, s, t):
        arrived(zref(r, a, d, s, t), ("z", r, a, d, s, t))
        if s < hops[a][d]:
            zsend(r, a, d, s + 1, t)

    def do_hs(a, t):
        arrived(xg.at[a, 1, own, lanes(t)], ("h", a, t))
        for d in range(2):
            zsend(1, a, d, 1, t)

    def do_start():
        for a in range(2):
            for t in range(ZT):
                send((x_in, g_in)[a].at[:, lanes(t)], xg.at[a, 1, own, lanes(t)], ("h", a, t), h_dev)
        for a in range(2):
            for t in range(ZT):
                for d in range(2):
                    zsend(0, a, d, 1, t)

    def piece(b):
        return pl.ds(b * CH, CH)

    def do_wstart(b):
        send(win.at[:, piece(b)], wi.at[3, :, piece(b)], ("w", b, 0), xp)
        send(win.at[:, piece(b)], wi.at[1, :, piece(b)], ("w", b, 2), xm)
        send(wout.at[piece(b), :], wo.at[3, piece(b), :], ("w", b, 1), xp)
        send(wout.at[piece(b), :], wo.at[1, piece(b), :], ("w", b, 3), xm)

    def do_wf(b, i):
        if i == 0:
            arrived(wi.at[3, :, piece(b)], ("w", b, 0))
            send(wi.at[3, :, piece(b)], wi.at[2, :, piece(b)], ("w", b, 4), xp)
        else:
            arrived(wo.at[1, piece(b), :], ("w", b, 3))
            send(wo.at[1, piece(b), :], wo.at[2, piece(b), :], ("w", b, 5), xm)

    own_w = []

    def w_here(s, b):
        if s == 1:
            arrived(wi.at[1, :, piece(b)], ("w", b, 2))
        elif s == 2:
            arrived(wi.at[2, :, piece(b)], ("w", b, 4))
            arrived(wo.at[2, piece(b), :], ("w", b, 5))
        elif s == 3:
            arrived(wo.at[3, piece(b), :], ("w", b, 1))

    def rows(i, n):
        return pl.ds(pl.multiple_of(i * n, n), n)

    def do_a(s, b, r):
        c = index(s, b, r)
        if not own_w:
            own_w.append(True)
            for copy in local:
                copy.wait()
        w_here(s, b)
        pre = dot(wi[s, :, b * CH : (b + 1) * CH], xg[0, r], 0, 0)
        back = dot(wo[s, b * CH : (b + 1) * CH, :], xg[1, r], 1, 0)
        for k, val in enumerate((pre, back)):
            pown[c, k] = val
            psend[c, k] = val.astype(BF)
        send(psend.at[c, :, rows(1 - cc, CH // 2), :], crecv.at[c], ("c", c), c_dev)

    def do_b(s, b, r):
        c = index(s, b, r)
        arrived(crecv.at[c], ("c", c))
        total = pown[c, :, rows(cc, CH // 2), :] + crecv[c].astype(F32)
        pown[c, :, : CH // 2, :] = total
        ysend[c] = total.astype(BF)
        send(ysend.at[c, :, rows(1 - b0, CH // 4), :], yrecv.at[c], ("y", c), y1_dev)

    def do_b2(s, b, r):
        c = index(s, b, r)
        arrived(yrecv.at[c], ("y", c))
        total = pown[c, :, rows(b0, CH // 4), :] + yrecv[c].astype(F32)
        pown[c, :, : CH // 4, :] = total
        y2send[c] = total.astype(BF)
        send(y2send.at[c, :, rows(1 - b1, CH // 8), :], y2recv.at[c], ("y2", c), y2_dev)

    def hrows(p0, p1):
        return rows(cc * 4 + p0 * 2 + p1, CH // 8)

    def do_c(s, b, r):
        c = index(s, b, r)
        arrived(y2recv.at[c], ("y2", c))
        total = pown[c, :, rows(b1, CH // 8), :] + y2recv[c].astype(F32)
        ht[c, hrows(b0, b1), :] = (total[1] * gelu_slope(total[0])).astype(BF)
        ref = ht.at[c, hrows(b0, b1), :]
        for k, dev in ((1, y1_dev), (2, y2_dev), (3, y3_dev)):
            send(ref, ref, ("ah", c, k), dev)

    def do_d(s, b, r):
        c = index(s, b, r)
        arrived(ht.at[c, : 3 * CH // 8, :], ("ah", c))
        ref = ht.at[c, rows(cc, CH // 2), :]
        send(ref, ref, ("ac", c), c_dev)

    first = [True, True]

    def do_e(s, b, r):
        c = index(s, b, r)
        arrived(ht.at[c, rows(1 - cc, CH // 2), :], ("ac", c))
        val = dot(wi[s, :, b * CH : (b + 1) * CH], ht[c], 1, 0)
        dxacc[r] = val if first[r] else dxacc[r] + val
        first[r] = False

    def do_dx(r):
        dxs[r] = dxacc[r].astype(BF)
        for k in (4, 3, 5, 2, 6, 1, 7):
            to = (z + k) % 8
            send(dxs.at[r, zrows(to), :], dxr.at[r, k - 1], ("dx", r, k), {"gz": to})

    def do_dw(s, b):
        dw = dot(xg[0, 0], ht[index(s, b, 0)], 1, 1) + dot(xg[0, 1], ht[index(s, b, 1)], 1, 1)
        if s == 0:
            dwf0[b] = dw
        elif s == 1:
            dwf[b, 0] = dw[:384]
            put_dw(b, 2, dw[384:], xp)
        elif s == 2:
            put_dw(b, 0, dw[:384], xp)
            put_dw(b, 1, dw[384:], xm)
        else:
            dwf[b, 1] = dw[384:]
            put_dw(b, 3, dw[:384], xm)

    def put_dw(b, i, val, dev):
        dws[b, i] = val.astype(BF)
        send(dws.at[b, i], dwr.at[b, i], ("dw", b, i), dev)

    def do_add(b, i):
        arrived(dwr.at[b, i], ("dw", b, i))
        put_dw(b, 4 + i, dwf[b, i] + dwr[b, i].astype(F32), xm if i else xp)

    def do_own(b):
        arrived(dwr.at[b, 2:], ("dw", b, 2))
        low = dwf0[b, :384] + dwr[b, 3].astype(F32) + dwr[b, 4].astype(F32)
        high = dwf0[b, 384:] + dwr[b, 2].astype(F32) + dwr[b, 5].astype(F32)
        dw_out[:384, b * CH : (b + 1) * CH] = low.astype(BF)
        dw_out[384:, b * CH : (b + 1) * CH] = high.astype(BF)

    scaled = {}

    def do_sq():
        scaled["w"] = (dw_out[...].astype(F32) * UP).astype(BF)

    def do_sq2():
        wf = dw_out[...].astype(F32)
        sqs[...] = jnp.broadcast_to(jnp.sum(wf * wf), (8, 128))
        for k in range(1, 8):
            send(sqs, sqr.at[k - 1], ("sq", k), {"gx": (gx + k) % 8})

    x1, x2, x3 = (xx + 1) % 4, (xx + 2) % 4, (xx + 3) % 4
    width = 768 // NP

    def put_g(p, i, val, dev):
        gsend[p, i] = val.astype(BF)
        send(gsend.at[p, i], grecv.at[p, i], ("g", p, i), dev)

    def do_g(p):
        ws = scaled["w"]
        gbuf[p] = dot(ws, ws[p * width : (p + 1) * width], 1, 1).reshape(2, 4, 96, width)
        if p == 0:
            gys[...] = gbuf[p, 1 - hi].astype(BF)
            send(gys, gyr, ("gy",), h_dev)
            return
        put_g(p, 0, gbuf[p, 0, x2], xp)
        put_g(p, 1, gbuf[p, 1, x2], xm)

    def do_gx(p):
        arrived(gyr, ("gy",))
        total = gbuf[p, hi] + gyr[...].astype(F32)
        gbuf[p, hi] = total
        g3s[...] = total.astype(BF)
        for k, to in ((2, x2), (1, x1), (3, x3)):
            send(g3s.at[to], g3r.at[k - 1], ("g3", k), {"gx": hi * 4 + to})

    def do_g2(p):
        put_g(p, 2, gbuf[p, 1, x1], xp)
        put_g(p, 3, gbuf[p, 0, x3], xm)

    def do_ga(p, i):
        arrived(grecv.at[p, i], ("g", p, i))
        mine = gbuf[p, 1, x3] if i else gbuf[p, 0, x1]
        put_g(p, 4 + i, mine + grecv[p, i].astype(F32), xm if i else xp)

    def do_go(p):
        arrived(grecv.at[p, 2:], ("g", p, 2))
        gbuf[p, 0, xx] = gbuf[p, 0, xx] + grecv[p, 3].astype(F32) + grecv[p, 4].astype(F32)
        gbuf[p, 1, xx] = gbuf[p, 1, xx] + grecv[p, 2].astype(F32) + grecv[p, 5].astype(F32)
        ghs[p] = gbuf[p, 1 - hi, xx].astype(BF)
        send(ghs.at[p], ghr.at[p], ("gh", p), h_dev)

    def do_gf(p):
        if "factor" not in scaled:
            sq = sqs[...]
            arrived(sqr, ("sq",))
            for k in range(1, 8):
                sq = sq + sqr[k - 1]
            scaled["factor"] = DOWN / (jnp.sqrt(sq[:1, :1]) + 1e-07)
        factor = scaled["factor"]
        val = gbuf[p, hi, xx]
        if p == 0:
            arrived(g3r, ("g3", 1))
            for k in range(3):
                val = val + g3r[k].astype(F32)
        else:
            arrived(ghr.at[p], ("gh", p))
            val = val + ghr[p].astype(F32)
        val = val * factor * factor * 768.0
        gram_out[:, p * width : (p + 1) * width] = val

    def do_dxs(r):
        total = dxacc[r, own, :]
        arrived(dxr.at[r], ("dx", r))
        for k in range(1, 8):
            total = total + dxr[r, k - 1].astype(F32)
        if r == 1:
            dxh[...] = total.astype(BF)
            send(dxh, dxhr, ("dxh",), h_dev)
        else:
            dxo[...] = total

    def do_dxf():
        arrived(dxhr, ("dxh",))
        dx_out[...] = (dxo[...] + dxhr[...].astype(F32)).astype(BF)

    steps = {
        "start": do_start, "wstart": do_wstart, "hs": do_hs, "z": do_z, "wf": do_wf,
        "A": do_a, "B": do_b, "B2": do_b2, "C": do_c, "D": do_d, "E": do_e, "dw": do_dw, "add": do_add, "own": do_own,
        "sq": do_sq, "sq2": do_sq2, "g": do_g, "gx": do_gx, "g2": do_g2, "ga": do_ga, "go": do_go, "gf": do_gf,
        "dx": do_dx, "dxs": do_dxs, "dxf": do_dxf,
    }
    for step in SCHEDULE:
        steps[step[0]](*step[1:])

    totals = {
        "h": xg.at[:, 0, :96, :], "z": xg.at[:, :, :672, :], "w0": wi.at[:3], "w1": wo.at[:3],
        "c": crecv, "y": yrecv, "y2": y2recv, "ah": ht.at[:, : 3 * CH // 8, :], "ac": ht.at[:, : CH // 2, :],
        "dw": dwr, "dx": dxr, "sq": sqr, "g": grecv.at[1:], "gh": ghr.at[1:], "gy": gyr, "g3": g3r, "dxh": dxhr,
    }
    for kind, ref in totals.items():
        k = kinds[kind]
        pltpu.make_async_remote_copy(
            src_ref=ref, dst_ref=ref, send_sem=s_all.at[k], recv_sem=r_all.at[0],
            device_id=c_dev, device_id_type=MESH,
        ).wait_send()


def hand_on(*refs):
    sem = refs[-1]
    copies = [pltpu.make_async_copy(refs[i], refs[6 + i], sem.at[i]) for i in range(3)]
    copies += [pltpu.make_async_copy(refs[6 + i], refs[3 + i], sem.at[3 + i]) for i in range(3)]
    for copy in copies[:3]:
        copy.start()
    for i in range(3):
        copies[i].wait()
        copies[3 + i].start()
    for copy in copies[3:]:
        copy.wait()


def body(inputs, out_grad, w_in, w_out):
    vmem = pl.BlockSpec(memory_space=pltpu.VMEM)
    hbm = pl.BlockSpec(memory_space=pl.ANY)
    dma = pltpu.SemaphoreType.DMA
    n = 8 * NH
    width = 768 // NP
    out_shape = (
        jax.ShapeDtypeStruct((96, 256), BF),
        jax.ShapeDtypeStruct((768, 256), BF),
        jax.ShapeDtypeStruct((96, 768), F32),
    )
    results = pl.pallas_call(
        kernel,
        out_shape=out_shape,
        in_specs=[hbm] * 4,
        out_specs=(vmem,) * 3,
        scratch_shapes=[
            pltpu.VMEM((2, 2, 768, 256), BF),
            pltpu.VMEM((4, 768, 256), BF),
            pltpu.VMEM((4, 256, 768), BF),
            pltpu.VMEM((n, 2, CH, 256), BF),
            pltpu.VMEM((n, 2, CH, 256), F32),
            pltpu.VMEM((n, 2, CH // 2, 256), BF),
            pltpu.VMEM((n, 2, CH // 2, 256), BF),
            pltpu.VMEM((n, 2, CH // 4, 256), BF),
            pltpu.VMEM((n, 2, CH // 4, 256), BF),
            pltpu.VMEM((n, 2, CH // 8, 256), BF),
            pltpu.VMEM((n, CH, 256), BF),
            pltpu.VMEM((2, 768, 256), F32),
            pltpu.VMEM((96, 256), F32),
            pltpu.VMEM((2, 768, 256), BF),
            pltpu.VMEM((2, 7, 96, 256), BF),
            pltpu.VMEM((96, 256), BF),
            pltpu.VMEM((96, 256), BF),
            pltpu.VMEM((NH, 2, 384, CH), F32),
            pltpu.VMEM((NH, 768, CH), F32),
            pltpu.VMEM((NH, 6, 384, CH), BF),
            pltpu.VMEM((NH, 6, 384, CH), BF),
            pltpu.VMEM((NP, 2, 4, 96, width), F32),
            pltpu.VMEM((NP, 6, 96, width), BF),
            pltpu.VMEM((NP, 6, 96, width), BF),
            pltpu.VMEM((NP, 96, width), BF),
            pltpu.VMEM((NP, 96, width), BF),
            pltpu.VMEM((4, 96, width), BF),
            pltpu.VMEM((4, 96, width), BF),
            pltpu.VMEM((4, 96, width), BF),
            pltpu.VMEM((3, 96, width), BF),
            pltpu.VMEM((8, 128), F32),
            pltpu.VMEM((7, 8, 128), F32),
            dma((4,)), dma((KINDS,)), dma((SLOTS,)),
        ],
        compiler_params=pltpu.CompilerParams(
            collective_id=0, has_side_effects=True, vmem_limit_bytes=60 * 1024 * 1024
        ),
        cost_estimate=pl.CostEstimate(
            flops=3_600_000_000, bytes_accessed=4_000_000, transcendentals=131072
        ),
    )(inputs.T, out_grad.T, w_in, w_out)
    dx_t, weight_grad, gram = pl.pallas_call(
        hand_on,
        out_shape=out_shape,
        in_specs=[hbm] * 3,
        out_specs=(hbm,) * 3,
        scratch_shapes=[pltpu.VMEM(v.shape, v.dtype) for v in out_shape] + [dma((6,))],
    )(*results)
    return (dx_t.T, weight_grad, gram[None])


def solution(mesh):
    placed = (
        P("gx", ("gy", "gz")),
        P("gx", ("gy", "gz")),
        P("gy", ("gx", "gz")),
        P(("gx", "gz"), "gy"),
    )
    return jax.shard_map(
        body,
        mesh=mesh,
        in_specs=placed,
        out_specs=(P("gx", ("gy", "gz")), P("gy", ("gx", "gz")), P("gz", ("gy", "gx"), None)),
        check_vma=False,
    )
```

```python
import jax
import jax.numpy as jnp
from jax import lax
from jax.experimental import pallas as pl
from jax.experimental.pallas import tpu as pltpu
from jax.sharding import PartitionSpec as P

GELU_COEF = 0.7978845608
BF = jnp.bfloat16
F32 = jnp.float32
MESH = pl.DeviceIdType.MESH
UP = float(2.0**30)
DOWN = float(2.0**-30)
NH = 2
CH = 256 // NH
NP = 6
KINDS = 17
ZT = 2
SLOTS = 184
TOGETHER = {"ah": 2, "dx": 2, "sq": 1, "g3": 1}
LATE = (2, 3, 4, 5)

SCHEDULE = [
    ("start",), ("wstart", 0), ("z", 0, 0, 1, 1, 0), ("z", 0, 0, 0, 1, 1), ("z", 0, 0, 0, 1, 0), ("z", 0, 1, 1, 1, 0),
    ("z", 0, 1, 0, 1, 0), ("z", 0, 1, 1, 1, 1), ("hs", 0, 0), ("z", 0, 0, 1, 1, 1), ("z", 0, 1, 0, 1, 1),
    ("hs", 0, 1), ("hs", 1, 0), ("z", 0, 0, 0, 2, 0), ("hs", 1, 1), ("wstart", 1), ("z", 0, 1, 1, 2, 1),
    ("z", 0, 1, 0, 2, 0), ("z", 0, 0, 0, 2, 1), ("z", 0, 0, 1, 2, 0), ("z", 0, 1, 1, 2, 0), ("z", 1, 0, 0, 1, 0),
    ("z", 1, 0, 1, 1, 0), ("z", 1, 0, 0, 1, 1), ("z", 1, 1, 1, 1, 0), ("z", 1, 1, 1, 1, 1), ("z", 0, 0, 1, 2, 1),
    ("z", 1, 1, 0, 1, 0), ("z", 0, 0, 0, 3, 0), ("wf", 0, 0), ("z", 0, 1, 1, 3, 1), ("z", 1, 1, 0, 1, 1),
    ("z", 1, 0, 1, 1, 1), ("z", 0, 1, 0, 2, 1), ("z", 0, 0, 1, 3, 0), ("z", 0, 1, 1, 3, 0), ("z", 0, 0, 0, 3, 1),
    ("wf", 0, 1), ("z", 1, 0, 0, 2, 0), ("z", 1, 0, 1, 2, 0), ("z", 1, 0, 0, 2, 1), ("z", 1, 1, 1, 2, 0),
    ("z", 1, 1, 1, 2, 1), ("z", 0, 1, 0, 3, 0), ("z", 0, 0, 0, 4, 0), ("z", 1, 1, 0, 2, 1), ("z", 0, 0, 1, 3, 1),
    ("z", 1, 0, 1, 2, 1), ("z", 0, 1, 1, 4, 1), ("z", 1, 1, 0, 2, 0), ("z", 0, 1, 1, 4, 0), ("z", 0, 1, 0, 3, 1),
    ("z", 0, 0, 0, 4, 1), ("A", 1, 0, 0), ("A", 3, 0, 0), ("z", 1, 0, 0, 3, 0), ("z", 1, 1, 1, 3, 0),
    ("z", 1, 0, 0, 3, 1), ("B", 1, 0, 0), ("z", 1, 1, 1, 3, 1), ("A", 0, 0, 0), ("B", 3, 0, 0), ("wf", 1, 1),
    ("A", 1, 1, 0), ("z", 1, 0, 1, 3, 1), ("z", 1, 0, 1, 3, 0), ("B", 0, 0, 0), ("z", 1, 1, 0, 3, 1), ("wf", 1, 0),
    ("A", 3, 1, 0), ("B", 1, 1, 0), ("z", 1, 0, 0, 4, 0), ("B", 3, 1, 0), ("z", 1, 1, 0, 3, 0), ("z", 1, 1, 1, 4, 0),
    ("z", 1, 0, 0, 4, 1), ("z", 1, 1, 1, 4, 1), ("A", 3, 0, 1), ("B2", 1, 0, 0), ("A", 1, 0, 1), ("B2", 3, 0, 0),
    ("B", 3, 0, 1), ("A", 2, 0, 1), ("B", 1, 0, 1), ("A", 2, 0, 0), ("B2", 1, 1, 0), ("A", 1, 1, 1), ("B", 2, 0, 1),
    ("A", 3, 1, 1), ("B", 2, 0, 0), ("B2", 3, 1, 0), ("A", 0, 1, 1), ("C", 1, 0, 0), ("B2", 3, 0, 1), ("B", 3, 1, 1),
    ("B2", 1, 0, 1), ("A", 2, 1, 1), ("A", 2, 1, 0), ("B2", 2, 0, 1), ("B", 2, 1, 1), ("B", 2, 1, 0), ("B2", 2, 0, 0),
    ("B", 1, 1, 1), ("C", 3, 0, 0), ("B", 0, 1, 1), ("B2", 3, 1, 1), ("C", 3, 0, 1), ("B2", 2, 1, 1), ("B2", 2, 1, 0),
    ("A", 0, 0, 1), ("C", 2, 0, 1), ("C", 2, 0, 0), ("B", 0, 0, 1), ("A", 0, 1, 0), ("C", 1, 0, 1), ("B2", 0, 1, 1),
    ("B2", 1, 1, 1), ("D", 3, 0, 0), ("D", 1, 0, 0), ("C", 2, 1, 1), ("C", 2, 1, 0), ("C", 3, 1, 1), ("B", 0, 1, 0),
    ("D", 2, 0, 1), ("B2", 0, 0, 1), ("C", 3, 1, 0), ("D", 2, 0, 0), ("C", 1, 1, 0), ("E", 3, 0, 0), ("E", 2, 0, 1),
    ("D", 3, 0, 1), ("E", 2, 0, 0), ("dw", 2, 0), ("C", 1, 1, 1), ("D", 1, 0, 1), ("B2", 0, 0, 0), ("E", 3, 0, 1),
    ("dw", 3, 0), ("E", 1, 0, 0), ("E", 1, 0, 1), ("dw", 1, 0), ("D", 2, 1, 1), ("C", 0, 1, 1), ("D", 2, 1, 0),
    ("D", 3, 1, 1), ("C", 0, 0, 1), ("E", 2, 1, 1), ("E", 2, 1, 0), ("dw", 2, 1), ("B2", 0, 1, 0), ("E", 3, 1, 1),
    ("D", 3, 1, 0), ("add", 0, 1), ("add", 0, 0), ("D", 1, 1, 1), ("E", 3, 1, 0), ("C", 0, 0, 0), ("D", 1, 1, 0),
    ("E", 1, 1, 1), ("dw", 3, 1), ("D", 0, 1, 1), ("E", 1, 1, 0), ("dw", 1, 1), ("D", 0, 0, 1), ("C", 0, 1, 0),
    ("E", 0, 1, 1), ("E", 0, 0, 1), ("dx", 1), ("add", 1, 0), ("add", 1, 1), ("D", 0, 0, 0), ("D", 0, 1, 0),
    ("E", 0, 0, 0), ("dw", 0, 0), ("E", 0, 1, 0), ("own", 0), ("dw", 0, 1), ("own", 1), ("sq",), ("g", 4), ("g", 0),
    ("g", 5), ("g", 3), ("g", 2), ("g2", 4), ("g", 1), ("dx", 0), ("ga", 4, 0), ("ga", 4, 1), ("g2", 5), ("ga", 5, 0),
    ("ga", 5, 1), ("g2", 2), ("dxs", 1), ("ga", 2, 0), ("ga", 2, 1), ("ga", 3, 1), ("g2", 3), ("ga", 3, 0), ("g2", 1),
    ("sq2",), ("ga", 1, 1), ("ga", 1, 0), ("go", 4), ("go", 5), ("go", 2), ("gx", 0), ("go", 3), ("go", 1), ("gf", 2),
    ("gf", 5), ("gf", 3), ("gf", 4), ("gf", 0), ("dxs", 0), ("dxf",), ("gf", 1),
]


def index(s, b, r):
    return (s * NH + b) * 2 + r


def gelu_slope(preact):
    inner = GELU_COEF * (preact + 0.044715 * preact * preact * preact)
    tanh_part = jnp.tanh(inner)
    return 0.5 * (1.0 + tanh_part) + 0.5 * preact * (1.0 - tanh_part * tanh_part) * GELU_COEF * (
        1.0 + 3.0 * 0.044715 * preact * preact
    )


def dot(a, b, ca, cb):
    return lax.dot_general(a, b, (((ca,), (cb,)), ((), ())), preferred_element_type=F32)


def kernel(
    x_in, g_in, win, wout, dx_out, dw_out, gram_out,
    xg, wi, wo, psend, pown, crecv, ysend, yrecv, y2send, y2recv, ht,
    dxacc, dxo, dxs, dxr, dxh, dxhr, dwf, dwf0, dws, dwr,
    gbuf, gsend, grecv, ghs, ghr, gys, gyr, g3s, g3r, sqs, sqr, l_sem, s_all, r_all,
):
    gx = lax.axis_index("gx")
    gy = lax.axis_index("gy")
    z = lax.axis_index("gz")
    hi, xx = gx // 4, gx % 4
    yy, cc = gy // 2, gy % 2
    b0, b1 = yy % 2, yy // 2
    xp = {"gx": hi * 4 + (xx + 1) % 4}
    xm = {"gx": hi * 4 + (xx + 3) % 4}
    h_dev = {"gx": (1 - hi) * 4 + xx}
    c_dev = {"gy": yy * 2 + 1 - cc}
    y1_dev = {"gy": (b1 * 2 + 1 - b0) * 2 + cc}
    y2_dev = {"gy": ((1 - b1) * 2 + b0) * 2 + cc}
    y3_dev = {"gy": ((1 - b1) * 2 + 1 - b0) * 2 + cc}
    zp, zm = {"gz": (z + 1) % 8}, {"gz": (z + 7) % 8}

    barrier = pltpu.get_barrier_semaphore()
    partners = [{"gx": (gx + k) % 8} for k in range(1, 8)]
    partners += [{"gz": (z + k) % 8} for k in range(1, 8)]
    partners += [c_dev, y1_dev, y2_dev, y3_dev]
    for dev in partners:
        pl.semaphore_signal(barrier, inc=1, device_id=dev, device_id_type=MESH)

    slots = {}
    kinds = {}

    def rc(src, dst, name, dev):
        kind = name[0] + str(name[2] % 2) if name[0] == "w" else name[0]
        group = name[: TOGETHER[name[0]]] if name[0] in TOGETHER else name
        if name[0] in ("dw", "g") and name[2] in LATE:
            group = name[:2]
        k = kinds.setdefault(kind, len(kinds))
        slot = slots.setdefault(group, len(slots))
        return pltpu.make_async_remote_copy(
            src_ref=src, dst_ref=dst, send_sem=s_all.at[k], recv_sem=r_all.at[slot],
            device_id=dev, device_id_type=MESH,
        )

    def send(src, dst, name, dev):
        rc(src, dst, name, dev).start()

    waited = set()

    def arrived(ref, name):
        if name not in waited:
            waited.add(name)
            rc(ref, ref, name, c_dev).wait_recv()

    def zrows(i):
        return pl.ds(pl.multiple_of(i * 96, 32), 96)

    own = zrows(z)
    local = [
        pltpu.make_async_copy(x_in, xg.at[0, 0, own, :], l_sem.at[0]),
        pltpu.make_async_copy(g_in, xg.at[1, 0, own, :], l_sem.at[1]),
        pltpu.make_async_copy(win, wi.at[0], l_sem.at[2]),
        pltpu.make_async_copy(wout, wo.at[0], l_sem.at[3]),
    ]
    for copy in local:
        copy.start()
    pl.semaphore_wait(barrier, len(partners))

    hops = ((4, 3), (3, 4))

    def lanes(t):
        return pl.ds(t * (256 // ZT), 256 // ZT)

    def zref(r, a, d, s, t):
        begun = (z + 8 - s) % 8 if d == 0 else (z + s) % 8
        return xg.at[a, r, zrows(begun), lanes(t)]

    def zsend(r, a, d, s, t):
        ref = zref(r, a, d, s - 1, t)
        src = (x_in, g_in)[a].at[:, lanes(t)] if r == 0 and s == 1 else ref
        send(src, ref, ("z", r, a, d, s, t), zp if d == 0 else zm)

    def do_z(r, a, d, s, t):
        arrived(zref(r, a, d, s, t), ("z", r, a, d, s, t))
        if s < hops[a][d]:
            zsend(r, a, d, s + 1, t)

    def do_hs(a, t):
        arrived(xg.at[a, 1, own, lanes(t)], ("h", a, t))
        for d in range(2):
            zsend(1, a, d, 1, t)

    def do_start():
        for a in range(2):
            for t in range(ZT):
                send((x_in, g_in)[a].at[:, lanes(t)], xg.at[a, 1, own, lanes(t)], ("h", a, t), h_dev)
        for a in range(2):
            for t in range(ZT):
                for d in range(2):
                    zsend(0, a, d, 1, t)

    def piece(b):
        return pl.ds(b * CH, CH)

    def do_wstart(b):
        send(win.at[:, piece(b)], wi.at[3, :, piece(b)], ("w", b, 0), xp)
        send(win.at[:, piece(b)], wi.at[1, :, piece(b)], ("w", b, 2), xm)
        send(wout.at[piece(b), :], wo.at[3, piece(b), :], ("w", b, 1), xp)
        send(wout.at[piece(b), :], wo.at[1, piece(b), :], ("w", b, 3), xm)

    def do_wf(b, i):
        if i == 0:
            arrived(wi.at[3, :, piece(b)], ("w", b, 0))
            send(wi.at[3, :, piece(b)], wi.at[2, :, piece(b)], ("w", b, 4), xp)
        else:
            arrived(wo.at[1, piece(b), :], ("w", b, 3))
            send(wo.at[1, piece(b), :], wo.at[2, piece(b), :], ("w", b, 5), xm)

    own_w = []

    def w_here(s, b):
        if s == 1:
            arrived(wi.at[1, :, piece(b)], ("w", b, 2))
        elif s == 2:
            arrived(wi.at[2, :, piece(b)], ("w", b, 4))
            arrived(wo.at[2, piece(b), :], ("w", b, 5))
        elif s == 3:
            arrived(wo.at[3, piece(b), :], ("w", b, 1))

    def rows(i, n):
        return pl.ds(pl.multiple_of(i * n, n), n)

    def do_a(s, b, r):
        c = index(s, b, r)
        if not own_w:
            own_w.append(True)
            for copy in local:
                copy.wait()
        w_here(s, b)
        pre = dot(wi[s, :, b * CH : (b + 1) * CH], xg[0, r], 0, 0)
        back = dot(wo[s, b * CH : (b + 1) * CH, :], xg[1, r], 1, 0)
        for k, val in enumerate((pre, back)):
            pown[c, k] = val
            psend[c, k] = val.astype(BF)
        send(psend.at[c, :, rows(1 - cc, CH // 2), :], crecv.at[c], ("c", c), c_dev)

    def do_b(s, b, r):
        c = index(s, b, r)
        arrived(crecv.at[c], ("c", c))
        total = pown[c, :, rows(cc, CH // 2), :] + crecv[c].astype(F32)
        pown[c, :, : CH // 2, :] = total
        ysend[c] = total.astype(BF)
        send(ysend.at[c, :, rows(1 - b0, CH // 4), :], yrecv.at[c], ("y", c), y1_dev)

    def do_b2(s, b, r):
        c = index(s, b, r)
        arrived(yrecv.at[c], ("y", c))
        total = pown[c, :, rows(b0, CH // 4), :] + yrecv[c].astype(F32)
        pown[c, :, : CH // 4, :] = total
        y2send[c] = total.astype(BF)
        send(y2send.at[c, :, rows(1 - b1, CH // 8), :], y2recv.at[c], ("y2", c), y2_dev)

    def hrows(p0, p1):
        return rows(cc * 4 + p0 * 2 + p1, CH // 8)

    def do_c(s, b, r):
        c = index(s, b, r)
        arrived(y2recv.at[c], ("y2", c))
        total = pown[c, :, rows(b1, CH // 8), :] + y2recv[c].astype(F32)
        ht[c, hrows(b0, b1), :] = (total[1] * gelu_slope(total[0])).astype(BF)
        ref = ht.at[c, hrows(b0, b1), :]
        for k, dev in ((1, y1_dev), (2, y2_dev), (3, y3_dev)):
            send(ref, ref, ("ah", c, k), dev)

    def do_d(s, b, r):
        c = index(s, b, r)
        arrived(ht.at[c, : 3 * CH // 8, :], ("ah", c))
        ref = ht.at[c, rows(cc, CH // 2), :]
        send(ref, ref, ("ac", c), c_dev)

    first = [True, True]

    def do_e(s, b, r):
        c = index(s, b, r)
        arrived(ht.at[c, rows(1 - cc, CH // 2), :], ("ac", c))
        val = dot(wi[s, :, b * CH : (b + 1) * CH], ht[c], 1, 0)
        dxacc[r] = val if first[r] else dxacc[r] + val
        first[r] = False

    def do_dx(r):
        dxs[r] = dxacc[r].astype(BF)
        for k in (4, 3, 5, 2, 6, 1, 7):
            to = (z + k) % 8
            send(dxs.at[r, zrows(to), :], dxr.at[r, k - 1], ("dx", r, k), {"gz": to})

    def do_dw(s, b):
        dw = dot(xg[0, 0], ht[index(s, b, 0)], 1, 1) + dot(xg[0, 1], ht[index(s, b, 1)], 1, 1)
        if s == 0:
            dwf0[b] = dw
        elif s == 1:
            dwf[b, 0] = dw[:384]
            put_dw(b, 2, dw[384:], xp)
        elif s == 2:
            put_dw(b, 0, dw[:384], xp)
            put_dw(b, 1, dw[384:], xm)
        else:
            dwf[b, 1] = dw[384:]
            put_dw(b, 3, dw[:384], xm)

    def put_dw(b, i, val, dev):
        dws[b, i] = val.astype(BF)
        send(dws.at[b, i], dwr.at[b, i], ("dw", b, i), dev)

    def do_add(b, i):
        arrived(dwr.at[b, i], ("dw", b, i))
        put_dw(b, 4 + i, dwf[b, i] + dwr[b, i].astype(F32), xm if i else xp)

    def do_own(b):
        arrived(dwr.at[b, 2:], ("dw", b, 2))
        low = dwf0[b, :384] + dwr[b, 3].astype(F32) + dwr[b, 4].astype(F32)
        high = dwf0[b, 384:] + dwr[b, 2].astype(F32) + dwr[b, 5].astype(F32)
        dw_out[:384, b * CH : (b + 1) * CH] = low.astype(BF)
        dw_out[384:, b * CH : (b + 1) * CH] = high.astype(BF)

    scaled = {}

    def do_sq():
        scaled["w"] = (dw_out[...].astype(F32) * UP).astype(BF)

    def do_sq2():
        wf = dw_out[...].astype(F32)
        sqs[...] = jnp.broadcast_to(jnp.sum(wf * wf), (8, 128))
        for k in range(1, 8):
            send(sqs, sqr.at[k - 1], ("sq", k), {"gx": (gx + k) % 8})

    x1, x2, x3 = (xx + 1) % 4, (xx + 2) % 4, (xx + 3) % 4
    width = 768 // NP

    def put_g(p, i, val, dev):
        gsend[p, i] = val.astype(BF)
        send(gsend.at[p, i], grecv.at[p, i], ("g", p, i), dev)

    def do_g(p):
        ws = scaled["w"]
        gbuf[p] = dot(ws, ws[p * width : (p + 1) * width], 1, 1).reshape(2, 4, 96, width)
        if p == 0:
            gys[...] = gbuf[p, 1 - hi].astype(BF)
            send(gys, gyr, ("gy",), h_dev)
            return
        put_g(p, 0, gbuf[p, 0, x2], xp)
        put_g(p, 1, gbuf[p, 1, x2], xm)

    def do_gx(p):
        arrived(gyr, ("gy",))
        total = gbuf[p, hi] + gyr[...].astype(F32)
        gbuf[p, hi] = total
        g3s[...] = total.astype(BF)
        for k, to in ((2, x2), (1, x1), (3, x3)):
            send(g3s.at[to], g3r.at[k - 1], ("g3", k), {"gx": hi * 4 + to})

    def do_g2(p):
        put_g(p, 2, gbuf[p, 1, x1], xp)
        put_g(p, 3, gbuf[p, 0, x3], xm)

    def do_ga(p, i):
        arrived(grecv.at[p, i], ("g", p, i))
        mine = gbuf[p, 1, x3] if i else gbuf[p, 0, x1]
        put_g(p, 4 + i, mine + grecv[p, i].astype(F32), xm if i else xp)

    def do_go(p):
        arrived(grecv.at[p, 2:], ("g", p, 2))
        gbuf[p, 0, xx] = gbuf[p, 0, xx] + grecv[p, 3].astype(F32) + grecv[p, 4].astype(F32)
        gbuf[p, 1, xx] = gbuf[p, 1, xx] + grecv[p, 2].astype(F32) + grecv[p, 5].astype(F32)
        ghs[p] = gbuf[p, 1 - hi, xx].astype(BF)
        send(ghs.at[p], ghr.at[p], ("gh", p), h_dev)

    def do_gf(p):
        if "factor" not in scaled:
            sq = sqs[...]
            arrived(sqr, ("sq",))
            for k in range(1, 8):
                sq = sq + sqr[k - 1]
            scaled["factor"] = DOWN / (jnp.sqrt(sq[:1, :1]) + 1e-07)
        factor = scaled["factor"]
        val = gbuf[p, hi, xx]
        if p == 0:
            arrived(g3r, ("g3", 1))
            for k in range(3):
                val = val + g3r[k].astype(F32)
        else:
            arrived(ghr.at[p], ("gh", p))
            val = val + ghr[p].astype(F32)
        val = val * factor * factor * 768.0
        gram_out[:, p * width : (p + 1) * width] = val

    def do_dxs(r):
        total = dxacc[r, own, :]
        arrived(dxr.at[r], ("dx", r))
        for k in range(1, 8):
            total = total + dxr[r, k - 1].astype(F32)
        if r == 1:
            dxh[...] = total.astype(BF)
            send(dxh, dxhr, ("dxh",), h_dev)
        else:
            dxo[...] = total

    def do_dxf():
        arrived(dxhr, ("dxh",))
        dx_out[...] = (dxo[...] + dxhr[...].astype(F32)).astype(BF)

    steps = {
        "start": do_start, "wstart": do_wstart, "hs": do_hs, "z": do_z, "wf": do_wf,
        "A": do_a, "B": do_b, "B2": do_b2, "C": do_c, "D": do_d, "E": do_e, "dw": do_dw, "add": do_add, "own": do_own,
        "sq": do_sq, "sq2": do_sq2, "g": do_g, "gx": do_gx, "g2": do_g2, "ga": do_ga, "go": do_go, "gf": do_gf,
        "dx": do_dx, "dxs": do_dxs, "dxf": do_dxf,
    }
    for step in SCHEDULE:
        steps[step[0]](*step[1:])

    totals = {
        "h": xg.at[:, 0, :96, :], "z": xg.at[:, :, :672, :], "w0": wi.at[:3], "w1": wo.at[:3],
        "c": crecv, "y": yrecv, "y2": y2recv, "ah": ht.at[:, : 3 * CH // 8, :], "ac": ht.at[:, : CH // 2, :],
        "dw": dwr, "dx": dxr, "sq": sqr, "g": grecv.at[1:], "gh": ghr.at[1:], "gy": gyr, "g3": g3r, "dxh": dxhr,
    }
    for kind, ref in totals.items():
        k = kinds[kind]
        pltpu.make_async_remote_copy(
            src_ref=ref, dst_ref=ref, send_sem=s_all.at[k], recv_sem=r_all.at[0],
            device_id=c_dev, device_id_type=MESH,
        ).wait_send()


def hand_on(*refs):
    sem = refs[-1]
    copies = [pltpu.make_async_copy(refs[i], refs[6 + i], sem.at[i]) for i in range(3)]
    copies += [pltpu.make_async_copy(refs[6 + i], refs[3 + i], sem.at[3 + i]) for i in range(3)]
    for copy in copies[:3]:
        copy.start()
    for i in range(3):
        copies[i].wait()
        copies[3 + i].start()
    for copy in copies[3:]:
        copy.wait()


def body(inputs, out_grad, w_in, w_out):
    vmem = pl.BlockSpec(memory_space=pltpu.VMEM)
    hbm = pl.BlockSpec(memory_space=pl.ANY)
    dma = pltpu.SemaphoreType.DMA
    n = 8 * NH
    width = 768 // NP
    out_shape = (
        jax.ShapeDtypeStruct((96, 256), BF),
        jax.ShapeDtypeStruct((768, 256), BF),
        jax.ShapeDtypeStruct((96, 768), F32),
    )
    results = pl.pallas_call(
        kernel,
        out_shape=out_shape,
        in_specs=[hbm] * 4,
        out_specs=(vmem,) * 3,
        scratch_shapes=[
            pltpu.VMEM((2, 2, 768, 256), BF),
            pltpu.VMEM((4, 768, 256), BF),
            pltpu.VMEM((4, 256, 768), BF),
            pltpu.VMEM((n, 2, CH, 256), BF),
            pltpu.VMEM((n, 2, CH, 256), F32),
            pltpu.VMEM((n, 2, CH // 2, 256), BF),
            pltpu.VMEM((n, 2, CH // 2, 256), BF),
            pltpu.VMEM((n, 2, CH // 4, 256), BF),
            pltpu.VMEM((n, 2, CH // 4, 256), BF),
            pltpu.VMEM((n, 2, CH // 8, 256), BF),
            pltpu.VMEM((n, CH, 256), BF),
            pltpu.VMEM((2, 768, 256), F32),
            pltpu.VMEM((96, 256), F32),
            pltpu.VMEM((2, 768, 256), BF),
            pltpu.VMEM((2, 7, 96, 256), BF),
            pltpu.VMEM((96, 256), BF),
            pltpu.VMEM((96, 256), BF),
            pltpu.VMEM((NH, 2, 384, CH), F32),
            pltpu.VMEM((NH, 768, CH), F32),
            pltpu.VMEM((NH, 6, 384, CH), BF),
            pltpu.VMEM((NH, 6, 384, CH), BF),
            pltpu.VMEM((NP, 2, 4, 96, width), F32),
            pltpu.VMEM((NP, 6, 96, width), BF),
            pltpu.VMEM((NP, 6, 96, width), BF),
            pltpu.VMEM((NP, 96, width), BF),
            pltpu.VMEM((NP, 96, width), BF),
            pltpu.VMEM((4, 96, width), BF),
            pltpu.VMEM((4, 96, width), BF),
            pltpu.VMEM((4, 96, width), BF),
            pltpu.VMEM((3, 96, width), BF),
            pltpu.VMEM((8, 128), F32),
            pltpu.VMEM((7, 8, 128), F32),
            dma((4,)), dma((KINDS,)), dma((SLOTS,)),
        ],
        compiler_params=pltpu.CompilerParams(
            collective_id=0, has_side_effects=True, vmem_limit_bytes=60 * 1024 * 1024
        ),
        cost_estimate=pl.CostEstimate(
            flops=3_600_000_000, bytes_accessed=4_000_000, transcendentals=131072
        ),
    )(inputs.T, out_grad.T, w_in, w_out)
    dx_t, weight_grad, gram = pl.pallas_call(
        hand_on,
        out_shape=out_shape,
        in_specs=[hbm] * 3,
        out_specs=(hbm,) * 3,
        scratch_shapes=[pltpu.VMEM(v.shape, v.dtype) for v in out_shape] + [dma((6,))],
    )(*results)
    return (dx_t.T, weight_grad, gram[None])


def solution(mesh):
    placed = (
        P("gx", ("gy", "gz")),
        P("gx", ("gy", "gz")),
        P("gy", ("gx", "gz")),
        P(("gx", "gz"), "gy"),
    )
    return jax.shard_map(
        body,
        mesh=mesh,
        in_specs=placed,
        out_specs=(P("gx", ("gy", "gz")), P("gy", ("gx", "gz")), P("gz", ("gy", "gx"), None)),
        check_vma=False,
    )
```
